512 devices in a mesh: seq: 64 (over z, x, y_lo), tensor: 8 (over y_hi, core).
Axes of the slice: x: 4, y: 8 (y_hi: 4, y_lo: 2; y = y_hi * 2 + y_lo), z: 8, core: 2. Of those that a mesh axis runs over, the one named last changes fastest.
Arguments:
- hidden_in: bfloat16 [8192, 8192], P('seq', 'tensor'), may hold values from -6 to 6
- query_base: bfloat16 [8192, 8192], P('seq', 'tensor'), may hold values from -6 to 6
- key_proj: bfloat16 [8192, 1024], P('seq', 'tensor'), may hold values from -6 to 6
- frozen_value_output: bfloat16 [8192, 1024], P('seq', 'tensor'), may hold values from -24 to 24
- down_query: bfloat16 [8, 8192], P(None, 'tensor'), may hold values from -0.0625 to 0.0625
- up_query: bfloat16 [8, 8192], P(None, 'tensor'), may hold values from -0.625 to 0.625
- down_value: bfloat16 [8, 8192], P(None, 'tensor'), may hold values from -0.0625 to 0.0625
- value_up_weight: bfloat16 [8, 1024], P(None, 'tensor'), may hold values from -0.625 to 0.625
- grad_out: bfloat16 [8192, 8192], P('seq', 'tensor'), may hold values from -0.0625 to 0.0625
Outputs:
- attended: bfloat16 [8192, 8192], P('seq', 'tensor')
- grad_down_query: float32 [8, 8192], P(None, 'tensor')
- grad_up_query: float32 [8, 8192], P(None, 'tensor')
- grad_down_value: float32 [8, 8192], P(None, 'tensor')
- grad_up_value: float32 [8, 1024], P(None, 'tensor')
The draws below stay inside these ranges and needn't reach their ends.
All inputs are finite; a program needn't handle non-finite values.
Results may differ from the reference program's by a relative error of at most 0.017.
Values may be sent and summed in bfloat16 or wider, within the bound.
A program may use at most 64 MiB of HBM per device.

```python
import jax
import jax.numpy as jnp
from jax import lax

D = 8192
QUERY_HEADS = 64
KEY_VALUE_HEADS = 8
HEAD_SIZE = 128
ADAPTER_RANK = 8
GROUP_TOKENS = 2048
SEQUENCE_TOKENS = 8192


def draw_query_base(key, part):
    key = jax.random.fold_in(key, 1)
    base_start = jnp.clip(jax.random.normal(key, (SEQUENCE_TOKENS, QUERY_HEADS * HEAD_SIZE)), -6.0, 6.0)
    return base_start.astype(jnp.bfloat16)


def draw_key_proj(key, part):
    key = jax.random.fold_in(key, 2)
    base_start = jnp.clip(jax.random.normal(key, (SEQUENCE_TOKENS, KEY_VALUE_HEADS * HEAD_SIZE)), -6.0, 6.0)
    return base_start.astype(jnp.bfloat16)


def levels(rng, shape, pieces, low, high):
    gain = 1.0
    for dim, blocks in pieces:
        draws = jax.random.uniform(jax.random.fold_in(jax.random.fold_in(rng, 6), dim), (blocks,), jnp.float32, low / len(pieces), high / len(pieces))
        gain = gain * jnp.repeat(jnp.exp(draws), shape[dim] // blocks).reshape((-1,) + (1,) * (len(shape) - 1 - dim))
    return gain


def centred(own_key, shape, width, most, pieces=(), kind=jnp.bfloat16):
    gain = levels(own_key, shape, pieces, -0.22, 0.18) if pieces else 1.0
    entries = jax.random.normal(own_key, shape, jnp.float32) * width * gain
    return jnp.minimum(jnp.maximum(entries, -most), most).astype(kind)


def setup_inputs(seed: int = 0) -> dict:
    seeds = jax.random.split(jax.random.key(seed), 10)
    return {
        "hidden_in": centred(seeds[0], (SEQUENCE_TOKENS, D), 1.0, 6.0, ((0, 64), (1, 8))),
        "query_base": draw_query_base(jax.random.fold_in(seeds[9], 71), 0),
        "key_proj": draw_key_proj(jax.random.fold_in(seeds[9], 71), 0),
        "frozen_value_output": centred(seeds[3], (SEQUENCE_TOKENS, KEY_VALUE_HEADS * HEAD_SIZE), 4.0, 24.0, ((0, 64), (1, 8))),
        "down_query": centred(seeds[4], (ADAPTER_RANK, D), D ** -0.5, 0.0625, ((1, 8),)),
        "up_query": centred(seeds[5], (ADAPTER_RANK, QUERY_HEADS * HEAD_SIZE), 0.1, 0.625, ((1, 8),)),
        "down_value": centred(seeds[6], (ADAPTER_RANK, D), D ** -0.5, 0.0625, ((1, 8),)),
        "value_up_weight": centred(seeds[7], (ADAPTER_RANK, KEY_VALUE_HEADS * HEAD_SIZE), 0.1, 0.625, ((1, 8),)),
        "grad_out": centred(seeds[8], (SEQUENCE_TOKENS, QUERY_HEADS * HEAD_SIZE), (SEQUENCE_TOKENS ** -0.5), 0.0625, ((0, 64), (1, 8))),
    }


adapter_gain = 2.0


def group_heads(query_group, key_group, value_group, cot_group):
    inv_root = HEAD_SIZE ** -0.5
    causal = jnp.tril(jnp.ones((GROUP_TOKENS, GROUP_TOKENS), dtype=bool))

    def single(packed):
        query_one, key_one, value_one, cot_one = packed
        key_f = key_one.astype(jnp.float32)
        value_f = value_one.astype(jnp.float32)
        cot_f = cot_one.astype(jnp.float32)
        scores = jnp.einsum("trd,ud->rtu", query_one.astype(jnp.float32), key_f) * inv_root
        row_max = jnp.max(jnp.where(causal, scores, -jnp.inf), axis=-1, keepdims=True)
        exp_terms = jnp.exp(jnp.where(causal, scores - row_max, -jnp.inf))
        soft_weights = exp_terms / jnp.sum(exp_terms, axis=-1, keepdims=True)
        rounded = lax.optimization_barrier(soft_weights.astype(jnp.bfloat16)).astype(jnp.float32)
        output = jnp.einsum("rtu,ud->trd", rounded, value_f)
        value_grad = jnp.einsum("rtu,trd->ud", rounded, cot_f)
        grad_probs = jnp.einsum("trd,ud->rtu", cot_f, value_f)
        center = jnp.sum(soft_weights * grad_probs, axis=-1, keepdims=True)
        grad_scores = soft_weights * (grad_probs - center)
        grad_round = lax.optimization_barrier(grad_scores.astype(jnp.bfloat16)).astype(jnp.float32)
        grad_query = jnp.einsum("rtu,ud->trd", grad_round, key_f) * inv_root
        return output.astype(jnp.bfloat16), grad_query, value_grad

    return lax.map(single, (query_group, key_group, value_group, cot_group))


def arrange(array, shift_offset, columns):
    rolled = jnp.roll(array, -shift_offset, axis=0)
    return rolled.reshape((SEQUENCE_TOKENS // GROUP_TOKENS, GROUP_TOKENS) + columns)


def restore(array, shift_offset):
    flat = array.reshape(SEQUENCE_TOKENS, -1)
    return jnp.roll(flat, shift_offset, axis=0)


def reference(hidden_in, query_base, key_proj, frozen_value_output, down_query, up_query, down_value, value_up_weight, grad_out):
    highest = lax.Precision.HIGHEST
    low_query = jnp.dot(hidden_in, down_query.T, preferred_element_type=jnp.float32)
    low_value = jnp.dot(hidden_in, down_value.T, preferred_element_type=jnp.float32)
    query = (query_base.astype(jnp.float32) + adapter_gain * jnp.dot(low_query, up_query.astype(jnp.float32), precision=highest)).astype(jnp.bfloat16)
    value = (frozen_value_output.astype(jnp.float32) + adapter_gain * jnp.dot(low_value, value_up_weight.astype(jnp.float32), precision=highest)).astype(jnp.bfloat16)
    repeat_count = QUERY_HEADS // KEY_VALUE_HEADS
    out_list = []
    grad_list = []
    value_list = []
    for key_value_index in range(KEY_VALUE_HEADS):
        shift_offset = GROUP_TOKENS // 2 if key_value_index >= KEY_VALUE_HEADS // 2 else 0
        query_cols = query[:, key_value_index * repeat_count * HEAD_SIZE:(key_value_index + 1) * repeat_count * HEAD_SIZE]
        cot_cols = grad_out[:, key_value_index * repeat_count * HEAD_SIZE:(key_value_index + 1) * repeat_count * HEAD_SIZE]
        key_cols = key_proj[:, key_value_index * HEAD_SIZE:(key_value_index + 1) * HEAD_SIZE]
        value_cols = value[:, key_value_index * HEAD_SIZE:(key_value_index + 1) * HEAD_SIZE]
        output, grad_query, value_grad = group_heads(
            arrange(query_cols, shift_offset, (repeat_count, HEAD_SIZE)),
            arrange(key_cols, shift_offset, (HEAD_SIZE,)),
            arrange(value_cols, shift_offset, (HEAD_SIZE,)),
            arrange(cot_cols, shift_offset, (repeat_count, HEAD_SIZE)))
        out_list.append(restore(output, shift_offset))
        grad_list.append(restore(grad_query, shift_offset))
        value_list.append(restore(value_grad, shift_offset))
    attended = jnp.concatenate(out_list, axis=1)
    d_query = jnp.concatenate(grad_list, axis=1)
    d_value = jnp.concatenate(value_list, axis=1)
    grad_up_query = adapter_gain * jnp.dot(low_query.T, d_query, precision=highest)
    grad_up_value = adapter_gain * jnp.dot(low_value.T, d_value, precision=highest)
    low_grad_query = (adapter_gain * jnp.dot(d_query, up_query.astype(jnp.float32).T, precision=highest)).astype(jnp.bfloat16)
    low_grad_value = (adapter_gain * jnp.dot(d_value, value_up_weight.astype(jnp.float32).T, precision=highest)).astype(jnp.bfloat16)
    grad_down_query = jnp.dot(low_grad_query.T, hidden_in, preferred_element_type=jnp.float32)
    grad_down_value = jnp.dot(low_grad_value.T, hidden_in, preferred_element_type=jnp.float32)
    return (attended, grad_down_query, grad_up_query, grad_down_value, grad_up_value)
```

```python
import functools
import math

import jax
import jax.numpy as jnp
from jax import lax
from jax.experimental import pallas as pl
from jax.experimental.pallas import tpu as pltpu
from jax.sharding import PartitionSpec as P

MESH = pl.DeviceIdType.MESH
GROUP_TOKENS = 2048
HEADS = 8
HEAD = 128
RANK = 8
TOK = 128
WIDTH = HEADS * HEAD
GAIN = 2.0
ROOT = HEAD ** -0.5
LOG2E = math.log2(math.e)
F32 = jnp.float32
BF16 = jnp.bfloat16
NT = (((1,), (1,)), ((), ()))


def dot(a, b):
    return jnp.dot(a, b, preferred_element_type=F32)


def dot_nt(a, b):
    return lax.dot_general(a, b, NT, preferred_element_type=F32)


def split2(x):
    hi = x.astype(BF16).astype(F32)
    return hi, x - hi


def kernel(
    n_seq, n_tensor, group,
    hid, qb, kp, fv, dq, uq, dv, uv, go,
    att, gdq, guq, gdv, guv,
    parts1, parts2, kbuf, vbuf, vown, lgout, lgin, ain, bin_, cin, aout,
    qs, sbuf, ebuf, dpbuf, stat, linv, oacc, dqacc, dol, dqhi, dqlo,
    p1s, p1r, ks, kf, kr, vs, vf, vr, ls, lr, p2s, p2r, asd, ard, bsd, brd, csd, crd,
):
    s = lax.axis_index("seq")
    t = lax.axis_index("tensor")
    chips = group // 2
    n_groups = n_seq // group
    wide = WIDTH // chips
    lag = jnp.where(t >= n_tensor // 2, group // 2, 0)
    rolled = lax.rem(s - lag + n_seq, n_seq)
    g = rolled // group
    p = lax.rem(rolled, group)
    c = p // 2
    yl = lax.rem(p, 2)
    mate = 2 * c + 1 - yl

    def place(gg, pp):
        return lax.rem(gg * group + pp + lag, n_seq)

    def dev(gg, pp):
        return (place(gg, pp), t)

    def remote(src, dst, send, recv, device):
        return pltpu.make_async_remote_copy(
            src_ref=src, dst_ref=dst, send_sem=send, recv_sem=recv,
            device_id=device, device_id_type=MESH,
        )

    barrier = pltpu.get_barrier_semaphore()

    def greet(device):
        pl.semaphore_signal(barrier, inc=1, device_id=device, device_id_type=MESH)

    def greet_tensor(i, carry):
        greet((s, lax.rem(t + i, n_tensor)))
        return carry

    def greet_group(i, carry):
        greet(dev(g, lax.rem(p + i, group)))
        return carry

    def greet_far(i, carry):
        greet(dev(lax.rem(g + 1 + i // 2, n_groups), 2 * c + lax.rem(i, 2)))
        return carry

    lax.fori_loop(1, n_tensor, greet_tensor, 0)
    lax.fori_loop(1, group, greet_group, 0)
    lax.fori_loop(0, 2 * (n_groups - 1), greet_far, 0)

    down = jnp.concatenate([dq[...].astype(F32), dv[...].astype(F32)], axis=0).astype(BF16)
    parts1[t] = dot_nt(down, hid[...])
    kbuf[p] = kp[...]

    pl.semaphore_wait(barrier, (n_tensor - 1) + (group - 1) + 2 * (n_groups - 1))

    def part1_copy(i):
        peer = lax.rem(t + i, n_tensor)
        return remote(parts1.at[t], parts1.at[t], p1s.at[i], p1r.at[t], (s, peer))

    def start_part1(i, carry):
        part1_copy(i).start()
        return carry

    lax.fori_loop(1, n_tensor, start_part1, 0)

    def k_copy(to):
        return remote(kp, kbuf.at[p], ks.at[to], kr.at[p], dev(g, 2 * to + yl))

    def k_pair(frm):
        return remote(kbuf.at[2 * frm + yl], kbuf.at[2 * frm + yl], kf.at[frm], kr.at[2 * frm + yl], dev(g, mate))

    def v_copy(to):
        return remote(vown, vbuf.at[p], vs.at[to], vr.at[p], dev(g, 2 * to + yl))

    def v_pair(frm):
        return remote(vbuf.at[2 * frm + yl], vbuf.at[2 * frm + yl], vf.at[frm], vr.at[2 * frm + yl], dev(g, mate))

    def k_wait(pp):
        pltpu.make_async_copy(kbuf.at[pp], kbuf.at[pp], kr.at[pp]).wait()

    def v_wait(pp):
        pltpu.make_async_copy(vbuf.at[pp], vbuf.at[pp], vr.at[pp]).wait()

    k_pair(c).start()

    def start_k(to, carry):
        k_copy(to).start()
        return carry

    lax.fori_loop(c + 1, chips, start_k, 0)

    def wait_part1(i, carry):
        src = lax.rem(t + i, n_tensor)
        pltpu.make_async_copy(parts1.at[src], parts1.at[src], p1r.at[src]).wait()
        return carry

    lax.fori_loop(1, n_tensor, wait_part1, 0)
    low = parts1[0]
    for i in range(1, n_tensor):
        low = low + parts1[i]
    hi = low.astype(BF16).astype(F32)
    rest = low - hi
    mid = rest.astype(BF16).astype(F32)
    lo = rest - mid
    zeros = jnp.zeros((TOK - 48, TOK), F32)
    pieces = jnp.transpose(jnp.concatenate([hi, mid, lo, zeros], axis=0)).astype(BF16)
    none_q = jnp.zeros((RANK, WIDTH), F32)
    none_v = jnp.zeros((RANK, HEAD), F32)
    uqf = uq[...].astype(F32)
    uvf = uv[...].astype(F32)
    up_v = jnp.concatenate([none_v, uvf] * 3 + [jnp.zeros((TOK - 48, HEAD), F32)], axis=0).astype(BF16)
    value = (fv[...].astype(F32) + GAIN * dot(pieces, up_v)).astype(BF16)
    low_v = jnp.concatenate([hi[RANK:], rest[RANK:]], axis=0).astype(BF16)
    vown[0:TOK, :] = value
    vown[TOK:TOK + 16, :] = low_v
    vbuf[p] = vown[...]

    v_pair(c).start()

    def start_v(to, carry):
        v_copy(to).start()
        return carry

    lax.fori_loop(c + 1, chips, start_v, 0)

    up_q = jnp.concatenate([uqf, none_q] * 3 + [jnp.zeros((TOK - 48, WIDTH), F32)], axis=0).astype(BF16)
    for h in range(HEADS):
        cols = slice(h * HEAD, (h + 1) * HEAD)
        qs[cols, :] = (qb[:, cols].astype(F32) + GAIN * dot(pieces, up_q[:, cols])).astype(BF16)

    def forward_k(i, carry):
        frm = c - 1 - i
        k_wait(2 * frm + yl)
        k_pair(frm).start()
        return carry

    def keys_of(ch):
        return kbuf[pl.ds(2 * ch, 2)].reshape(2 * TOK, HEAD)

    lax.fori_loop(0, c, forward_k, 0)
    k_wait(mate)
    kc = keys_of(c)
    column = lax.broadcasted_iota(jnp.int32, (TOK, 2 * TOK), 1)
    row = lax.broadcasted_iota(jnp.int32, (TOK, 2 * TOK), 0)
    allowed = column <= row + yl * TOK
    for h in range(HEADS):
        rows = slice(h * TOK, (h + 1) * TOK)
        sc = jnp.where(allowed, dot_nt(qs[rows, :], kc) * (ROOT * LOG2E), -1e30)
        sbuf[c, rows, :] = sc
        stat[rows, :] = jnp.maximum(sc[:, :TOK], sc[:, TOK:])

    def scores(i, carry):
        ch = c - 1 - i
        k_wait(2 * ch + 1 - yl)
        kc = keys_of(ch)
        for h in range(HEADS):
            rows = slice(h * TOK, (h + 1) * TOK)
            sc = dot_nt(qs[rows, :], kc) * (ROOT * LOG2E)
            sbuf[ch, rows, :] = sc
            stat[rows, :] = jnp.maximum(stat[rows, :], jnp.maximum(sc[:, :TOK], sc[:, TOK:]))
        return carry

    lax.fori_loop(0, c, scores, 0)
    for h in range(HEADS):
        rows = slice(h * TOK, (h + 1) * TOK)
        stat[rows, :] = jnp.broadcast_to(jnp.max(stat[rows, :], axis=1, keepdims=True), (TOK, HEAD))
    linv[...] = jnp.zeros_like(linv)

    def exps(i, carry):
        ch = c - i

        @pl.when(i > 0)
        def _():
            v_wait(2 * ch + yl)
            v_pair(ch).start()

        for h in range(HEADS):
            rows = slice(h * TOK, (h + 1) * TOK)
            m = stat[rows, :]
            e0 = jnp.exp2(sbuf[ch, rows, 0:TOK] - m)
            e1 = jnp.exp2(sbuf[ch, rows, TOK:2 * TOK] - m)
            linv[rows, :] += e0 + e1
            ebuf[ch, rows, 0:TOK] = e0.astype(BF16)
            ebuf[ch, rows, TOK:2 * TOK] = e1.astype(BF16)
        return carry

    lax.fori_loop(0, c + 1, exps, 0)
    for h in range(HEADS):
        rows = slice(h * TOK, (h + 1) * TOK)
        inv = 1.0 / jnp.sum(linv[rows, :], axis=1, keepdims=True)
        linv[rows, :] = jnp.broadcast_to(inv, (TOK, HEAD))
        dol[rows, :] = (go[:, rows].astype(F32) * inv).astype(BF16)

    weights = dot_nt(uv[...], dol[...])
    w_hi, w_lo = split2(weights)
    w16 = jnp.concatenate([w_hi, w_lo], axis=0).astype(BF16)

    def lg_copy(to):
        return remote(lgout.at[to], lgin.at[p], ls.at[to], lr.at[p], dev(g, to))

    def grads(i, carry):
        ch = c - i
        both = dot(w16, ebuf[ch])
        lg = GAIN * (both[0:RANK] + both[RANK:2 * RANK])
        lgout[2 * ch] = lg[:, 0:TOK]
        lgout[2 * ch + 1] = lg[:, TOK:2 * TOK]

        @pl.when(2 * ch < p)
        def _():
            lg_copy(2 * ch).start()

        @pl.when(2 * ch + 1 < p)
        def _():
            lg_copy(2 * ch + 1).start()

        return carry

    lax.fori_loop(0, c + 1, grads, 0)

    oacc[...] = jnp.zeros_like(oacc)
    dqacc[...] = jnp.zeros_like(dqacc)

    def outs(i, tt):
        ch = c - i
        v_wait(2 * ch + 1 - yl)
        vc = jnp.concatenate([vbuf[2 * ch, 0:TOK, :], vbuf[2 * ch + 1, 0:TOK, :]], axis=0)
        lows = jnp.concatenate([vbuf[2 * ch, TOK:TOK + 16, :], vbuf[2 * ch + 1, TOK:TOK + 16, :]], axis=1)
        for h in range(HEADS):
            rows = slice(h * TOK, (h + 1) * TOK)
            oacc[rows, :] += dot(ebuf[ch, rows, :], vc)
            dpbuf[ch, rows, :] = dot_nt(go[:, rows], vc)
        return tt + dot_nt(lows, ebuf[ch])

    tt = lax.fori_loop(0, c + 1, outs, jnp.zeros((16, HEADS * TOK), F32))
    for h in range(HEADS):
        rows = slice(h * TOK, (h + 1) * TOK)
        o = oacc[rows, :] * linv[rows, :]
        att[:, rows] = o.astype(BF16)
        center = jnp.sum(o * go[:, rows].astype(F32), axis=1, keepdims=True)
        stat[rows, :] = jnp.broadcast_to(center, (TOK, HEAD))

    def dquery(i, carry):
        ch = c - i
        kc = keys_of(ch)
        for h in range(HEADS):
            rows = slice(h * TOK, (h + 1) * TOK)
            cen = stat[rows, :]
            d0 = ebuf[ch, rows, 0:TOK].astype(F32) * (dpbuf[ch, rows, 0:TOK] - cen)
            d1 = ebuf[ch, rows, TOK:2 * TOK].astype(F32) * (dpbuf[ch, rows, TOK:2 * TOK] - cen)
            dqacc[rows, :] += dot(jnp.concatenate([d0.astype(BF16), d1.astype(BF16)], axis=1), kc)
        return carry

    lax.fori_loop(0, c + 1, dquery, 0)
    for h in range(HEADS):
        rows = slice(h * TOK, (h + 1) * TOK)
        d_hi, d_lo = split2(dqacc[rows, :] * (linv[rows, :] * ROOT))
        dqhi[:, rows] = d_hi.astype(BF16)
        dqlo[:, rows] = d_lo.astype(BF16)
    lgq = GAIN * (dot_nt(uq[...], dqhi[...]) + dot_nt(uq[...], dqlo[...]))

    def wait_lg(pp, acc):
        pltpu.make_async_copy(lgin.at[pp], lgin.at[pp], lr.at[pp]).wait()
        return acc + lgin[pp]

    lgv = lax.fori_loop(p + 1, group, wait_lg, lgout[p])
    parts2[t] = jnp.concatenate([lgq, lgv], axis=0)

    def part2_copy(i):
        peer = lax.rem(t + i, n_tensor)
        return remote(parts2.at[t], parts2.at[t], p2s.at[i], p2r.at[t], (s, peer))

    def start_part2(i, carry):
        part2_copy(i).start()
        return carry

    lax.fori_loop(1, n_tensor, start_part2, 0)

    lq16 = jnp.concatenate([hi[:RANK], rest[:RANK]], axis=0).astype(BF16)
    g_up = dot(lq16, dqhi[...])
    g_lo = dot(lq16, dqlo[...])
    g_up_q = GAIN * (g_up[:RANK] + g_up[RANK:] + g_lo[:RANK])
    t_hi, t_lo = split2(tt[:RANK] + tt[RANK:])
    g_v = dot(jnp.concatenate([t_hi, t_lo], axis=0).astype(BF16), dol[...])
    g_up_v = GAIN * (g_v[:RANK] + g_v[RANK:])
    rank_row = lax.broadcasted_iota(jnp.int32, (RANK, HEAD), 0)
    for k in range(chips):
        aout[k, RANK:2 * RANK, :] = g_up_q[:, k * wide:(k + 1) * wide]
        if wide > HEAD:
            aout[k, 3 * RANK:4 * RANK, :] = jnp.zeros((RANK, wide), F32)
        aout[k, 3 * RANK:4 * RANK, 0:HEAD] = jnp.where(lax.rem(rank_row, chips) == k, g_up_v, 0.0)

    def wait_part2(i, carry):
        src = lax.rem(t + i, n_tensor)
        pltpu.make_async_copy(parts2.at[src], parts2.at[src], p2r.at[src]).wait()
        return carry

    lax.fori_loop(1, n_tensor, wait_part2, 0)
    lowg = parts2[0]
    for i in range(1, n_tensor):
        lowg = lowg + parts2[i]
    g_down = dot(lowg.astype(BF16), hid[...])
    for k in range(chips):
        aout[k, 0:RANK, :] = g_down[0:RANK, k * wide:(k + 1) * wide]
        aout[k, 2 * RANK:3 * RANK, :] = g_down[RANK:2 * RANK, k * wide:(k + 1) * wide]

    def a_copy(i):
        to = lax.rem(c + i, chips)
        return remote(aout.at[to], ain.at[c], asd.at[i], ard.at[c], dev(g, 2 * to + yl))

    def c_copy(i):
        to = lax.rem(c + i, chips)
        return remote(cin.at[c], cin.at[c], csd.at[i], crd.at[c], dev(g, 2 * to + yl))

    mine = 2 * g + yl

    def b_copy(i):
        slot = lax.rem(mine + i, 2 * n_groups)
        return remote(
            bin_.at[mine], bin_.at[mine], bsd.at[i], brd.at[mine],
            dev(slot // 2, 2 * c + lax.rem(slot, 2)),
        )

    def start_a(i, carry):
        a_copy(i).start()
        return carry

    def start_b(i, carry):
        b_copy(i).start()
        return carry

    def start_c(i, carry):
        c_copy(i).start()
        return carry

    def waiter(buf, sem, me, count):
        def body(i, carry):
            src = lax.rem(me + i, count)
            pltpu.make_async_copy(buf.at[src], buf.at[src], sem.at[src]).wait()
            return carry

        lax.fori_loop(1, count, body, 0)

    lax.fori_loop(1, chips, start_a, 0)
    ain[c] = aout[c]
    waiter(ain, ard, c, chips)
    total = ain[0]
    for k in range(1, chips):
        total = total + ain[k]
    bin_[mine] = total
    lax.fori_loop(1, 2 * n_groups, start_b, 0)
    waiter(bin_, brd, mine, 2 * n_groups)
    total = bin_[0]
    for k in range(1, 2 * n_groups):
        total = total + bin_[k]
    cin[c] = total
    lax.fori_loop(1, chips, start_c, 0)
    waiter(cin, crd, c, chips)
    up_total = jnp.zeros((RANK, HEAD), F32)
    for k in range(chips):
        gdq[:, k * wide:(k + 1) * wide] = cin[k, 0:RANK, :]
        guq[:, k * wide:(k + 1) * wide] = cin[k, RANK:2 * RANK, :]
        gdv[:, k * wide:(k + 1) * wide] = cin[k, 2 * RANK:3 * RANK, :]
        up_total = up_total + cin[k, 3 * RANK:4 * RANK, 0:HEAD]
    guv[...] = up_total

    def end_tensor(i, carry):
        part1_copy(i).wait_send()
        part2_copy(i).wait_send()
        return carry

    def end_later(to, carry):
        k_copy(to).wait_send()
        v_copy(to).wait_send()
        return carry

    def end_pair(frm, carry):
        k_pair(frm).wait_send()
        v_pair(frm).wait_send()
        return carry

    def end_lg(to, carry):
        lg_copy(to).wait_send()
        return carry

    def end_row(i, carry):
        a_copy(i).wait_send()
        c_copy(i).wait_send()
        return carry

    def end_far(i, carry):
        b_copy(i).wait_send()
        return carry

    lax.fori_loop(1, n_tensor, end_tensor, 0)
    lax.fori_loop(c + 1, chips, end_later, 0)
    lax.fori_loop(0, c + 1, end_pair, 0)
    lax.fori_loop(0, p, end_lg, 0)
    lax.fori_loop(1, chips, end_row, 0)
    lax.fori_loop(1, 2 * n_groups, end_far, 0)


def solution(mesh, group_tokens=GROUP_TOKENS):
    n_seq, n_tensor = mesh.shape["seq"], mesh.shape["tensor"]
    group = group_tokens // TOK
    chips = group // 2
    far = 2 * (n_seq // group)
    wide = WIDTH // chips
    rows = HEADS * TOK
    vmem = pl.BlockSpec(memory_space=pltpu.VMEM)
    dma = pltpu.SemaphoreType.DMA

    def per_device(*args):
        return pl.pallas_call(
            functools.partial(kernel, n_seq, n_tensor, group),
            out_shape=(
                jax.ShapeDtypeStruct((TOK, WIDTH), BF16),
                jax.ShapeDtypeStruct((RANK, WIDTH), F32),
                jax.ShapeDtypeStruct((RANK, WIDTH), F32),
                jax.ShapeDtypeStruct((RANK, WIDTH), F32),
                jax.ShapeDtypeStruct((RANK, HEAD), F32),
            ),
            in_specs=[vmem] * 9,
            out_specs=(vmem,) * 5,
            scratch_shapes=[
                pltpu.VMEM((n_tensor, 2 * RANK, TOK), F32),
                pltpu.VMEM((n_tensor, 2 * RANK, TOK), F32),
                pltpu.VMEM((group, TOK, HEAD), BF16),
                pltpu.VMEM((group, TOK + 16, HEAD), BF16),
                pltpu.VMEM((TOK + 16, HEAD), BF16),
                pltpu.VMEM((group, RANK, TOK), F32),
                pltpu.VMEM((group, RANK, TOK), F32),
                pltpu.VMEM((chips, 4 * RANK, wide), F32),
                pltpu.VMEM((far, 4 * RANK, wide), F32),
                pltpu.VMEM((chips, 4 * RANK, wide), F32),
                pltpu.VMEM((chips, 4 * RANK, wide), F32),
                pltpu.VMEM((rows, HEAD), BF16),
                pltpu.VMEM((chips, rows, 2 * TOK), F32),
                pltpu.VMEM((chips, rows, 2 * TOK), BF16),
                pltpu.VMEM((chips, rows, 2 * TOK), F32),
                pltpu.VMEM((rows, HEAD), F32),
                pltpu.VMEM((rows, HEAD), F32),
                pltpu.VMEM((rows, HEAD), F32),
                pltpu.VMEM((rows, HEAD), F32),
                pltpu.VMEM((rows, HEAD), BF16),
                pltpu.VMEM((TOK, WIDTH), BF16),
                pltpu.VMEM((TOK, WIDTH), BF16),
                dma((n_tensor,)), dma((n_tensor,)),
                dma((chips,)), dma((chips,)), dma((group,)),
                dma((chips,)), dma((chips,)), dma((group,)),
                dma((group,)), dma((group,)),
                dma((n_tensor,)), dma((n_tensor,)),
                dma((chips,)), dma((chips,)),
                dma((far,)), dma((far,)),
                dma((chips,)), dma((chips,)),
            ],
            compiler_params=pltpu.CompilerParams(
                collective_id=0, has_side_effects=True, vmem_limit_bytes=48 * 1024 * 1024
            ),
        )(*args)

    split = P("seq", "tensor")
    cols = P(None, "tensor")
    return jax.shard_map(
        per_device,
        mesh=mesh,
        in_specs=(split, split, split, split, cols, cols, cols, cols, split),
        out_specs=(split, cols, cols, cols, cols),
        check_vma=False,
    )
```

```python
import functools
import math

import jax
import jax.numpy as jnp
from jax import lax
from jax.experimental import pallas as pl
from jax.experimental.pallas import tpu as pltpu
from jax.sharding import PartitionSpec as P

MESH = pl.DeviceIdType.MESH
GROUP_TOKENS = 2048
HEADS = 8
HEAD = 128
RANK = 8
TOK = 128
WIDTH = HEADS * HEAD
GAIN = 2.0
ROOT = HEAD ** -0.5
LOG2E = math.log2(math.e)
F32 = jnp.float32
BF16 = jnp.bfloat16
NT = (((1,), (1,)), ((), ()))


def dot(a, b):
    return jnp.dot(a, b, preferred_element_type=F32)


def dot_nt(a, b):
    return lax.dot_general(a, b, NT, preferred_element_type=F32)


def split2(x):
    hi = x.astype(BF16).astype(F32)
    return hi, x - hi


def arrived(buf, sem):
    pltpu.make_async_copy(buf, buf, sem).wait()


def kernel(
    n_seq, n_tensor, group,
    hid_h, qb_h, kp_h, fv_h, dq_h, uq_h, dv_h, uv_h, go_h,
    att_h, gdq_h, guq_h, gdv_h, guv_h,
    att, gdq, guq, gdv, guv, unload,
    hid, qb, kp, fv, dq, uq, dv, uv, go, load,
    parts1, parts2, kbuf, vbuf, vown, lgout, lgin, ain, bin_, cin, aout,
    qs, sbuf, ebuf, dpbuf, stat, linv, oacc, dqacc, dol, dqhi, dqlo,
    p1s, p1r, ks, kf, kr, vs, vf, vr, ls, lr, p2s, p2r, asd, ard, bsd, brd, csd, crd,
):
    s = lax.axis_index("seq")
    t = lax.axis_index("tensor")
    chips = group // 2
    n_groups = n_seq // group
    wide = WIDTH // chips
    lag = jnp.where(t >= n_tensor // 2, group // 2, 0)
    rolled = lax.rem(s - lag + n_seq, n_seq)
    g = rolled // group
    p = lax.rem(rolled, group)
    c = p // 2
    yl = lax.rem(p, 2)
    mate = 2 * c + 1 - yl

    def place(gg, pp):
        return lax.rem(gg * group + pp + lag, n_seq)

    def dev(gg, pp):
        return (place(gg, pp), t)

    def remote(src, dst, send, recv, device):
        return pltpu.make_async_remote_copy(
            src_ref=src, dst_ref=dst, send_sem=send, recv_sem=recv,
            device_id=device, device_id_type=MESH,
        )

    loads = [
        pltpu.make_async_copy(src, dst, load.at[i])
        for i, (src, dst) in enumerate((
            (hid_h, hid), (dq_h, dq), (dv_h, dv), (kp_h, kp), (fv_h, fv), (uv_h, uv), (uq_h, uq), (qb_h, qb), (go_h, go),
        ))
    ]
    for copy in loads[:4]:
        copy.start()

    barrier = pltpu.get_barrier_semaphore()

    def greet(device):
        pl.semaphore_signal(barrier, inc=1, device_id=device, device_id_type=MESH)

    def greet_tensor(i, carry):
        greet((s, lax.rem(t + i, n_tensor)))
        return carry

    def greet_group(i, carry):
        greet(dev(g, lax.rem(p + i, group)))
        return carry

    def greet_far(i, carry):
        greet(dev(lax.rem(g + 1 + i // 2, n_groups), 2 * c + lax.rem(i, 2)))
        return carry

    lax.fori_loop(1, n_tensor, greet_tensor, 0)
    lax.fori_loop(1, group, greet_group, 0)
    lax.fori_loop(0, 2 * (n_groups - 1), greet_far, 0)

    for copy in loads[4:]:
        copy.start()
    for copy in loads[:4]:
        copy.wait()

    down = jnp.concatenate([dq[...].astype(F32), dv[...].astype(F32)], axis=0).astype(BF16)
    parts1[t] = dot_nt(down, hid[...])
    kbuf[p] = kp[...]

    pl.semaphore_wait(barrier, (n_tensor - 1) + (group - 1) + 2 * (n_groups - 1))

    def part1_copy(i):
        peer = lax.rem(t + i, n_tensor)
        return remote(parts1.at[t], parts1.at[t], p1s.at[i], p1r.at[t], (s, peer))

    def start_part1(i, carry):
        part1_copy(i).start()
        return carry

    lax.fori_loop(1, n_tensor, start_part1, 0)

    def k_copy(to):
        return remote(kp, kbuf.at[p], ks.at[to], kr.at[p], dev(g, 2 * to + yl))

    def k_pair(frm):
        return remote(kbuf.at[2 * frm + yl], kbuf.at[2 * frm + yl], kf.at[frm], kr.at[2 * frm + yl], dev(g, mate))

    def v_copy(to):
        return remote(vown, vbuf.at[p], vs.at[to], vr.at[p], dev(g, 2 * to + yl))

    def v_pair(frm):
        return remote(vbuf.at[2 * frm + yl], vbuf.at[2 * frm + yl], vf.at[frm], vr.at[2 * frm + yl], dev(g, mate))

    def k_wait(pp):
        arrived(kbuf.at[pp], kr.at[pp])

    def v_wait(pp):
        arrived(vbuf.at[pp], vr.at[pp])

    k_pair(c).start()

    def start_k(to, carry):
        k_copy(chips - 1 - to).start()
        return carry

    lax.fori_loop(0, chips - 1 - c, start_k, 0)

    for copy in loads[4:]:
        copy.wait()

    def forward_k(i, carry):
        frm = c - 1 - i
        k_wait(2 * frm + yl)
        k_pair(frm).start()
        return carry

    lax.fori_loop(0, c, forward_k, 0)

    def wait_part1(i, carry):
        src = lax.rem(t + i, n_tensor)
        arrived(parts1.at[src], p1r.at[src])
        return carry

    lax.fori_loop(1, n_tensor, wait_part1, 0)
    low = parts1[0]
    for i in range(1, n_tensor):
        low = low + parts1[i]
    hi = low.astype(BF16).astype(F32)
    rest = low - hi
    mid = rest.astype(BF16).astype(F32)
    lo = rest - mid
    zeros = jnp.zeros((TOK - 48, TOK), F32)
    pieces = jnp.transpose(jnp.concatenate([hi, mid, lo, zeros], axis=0)).astype(BF16)
    none_q = jnp.zeros((RANK, WIDTH), F32)
    none_v = jnp.zeros((RANK, HEAD), F32)
    uqf = uq[...].astype(F32)
    uvf = uv[...].astype(F32)
    up_v = jnp.concatenate([none_v, uvf] * 3 + [jnp.zeros((TOK - 48, HEAD), F32)], axis=0).astype(BF16)
    value = (fv[...].astype(F32) + GAIN * dot(pieces, up_v)).astype(BF16)
    low_v = jnp.concatenate([hi[RANK:], rest[RANK:]], axis=0).astype(BF16)
    vown[0:TOK, :] = value
    vown[TOK:TOK + 16, :] = low_v
    vbuf[p] = vown[...]

    v_pair(c).start()

    def start_v(to, carry):
        v_copy(chips - 1 - to).start()
        return carry

    lax.fori_loop(0, chips - 1 - c, start_v, 0)

    up_q = jnp.concatenate([uqf, none_q] * 3 + [jnp.zeros((TOK - 48, WIDTH), F32)], axis=0).astype(BF16)
    for h in range(HEADS):
        cols = slice(h * HEAD, (h + 1) * HEAD)
        qs[cols, :] = (qb[:, cols].astype(F32) + GAIN * dot(pieces, up_q[:, cols])).astype(BF16)

    def keys_of(ch):
        return kbuf[pl.ds(2 * ch, 2)].reshape(2 * TOK, HEAD)

    k_wait(mate)
    kc = keys_of(c)
    column = lax.broadcasted_iota(jnp.int32, (TOK, 2 * TOK), 1)
    row = lax.broadcasted_iota(jnp.int32, (TOK, 2 * TOK), 0)
    allowed = column <= row + yl * TOK
    for h in range(HEADS):
        rows = slice(h * TOK, (h + 1) * TOK)
        sc = jnp.where(allowed, dot_nt(qs[rows, :], kc) * (ROOT * LOG2E), -1e30)
        sbuf[c, rows, :] = sc
        stat[rows, :] = jnp.maximum(sc[:, :TOK], sc[:, TOK:])

    def scores(i, carry):
        ch = c - 1 - i
        k_wait(2 * ch + 1 - yl)
        kc = keys_of(ch)
        for h in range(HEADS):
            rows = slice(h * TOK, (h + 1) * TOK)
            sc = dot_nt(qs[rows, :], kc) * (ROOT * LOG2E)
            sbuf[ch, rows, :] = sc
            stat[rows, :] = jnp.maximum(stat[rows, :], jnp.maximum(sc[:, :TOK], sc[:, TOK:]))
        return carry

    lax.fori_loop(0, c, scores, 0)
    for h in range(HEADS):
        rows = slice(h * TOK, (h + 1) * TOK)
        stat[rows, :] = jnp.broadcast_to(jnp.max(stat[rows, :], axis=1, keepdims=True), (TOK, HEAD))
    linv[...] = jnp.zeros_like(linv)

    def exps(i, carry):
        ch = c - i

        @pl.when(i > 0)
        def _():
            v_wait(2 * ch + yl)
            v_pair(ch).start()

        for h in range(HEADS):
            rows = slice(h * TOK, (h + 1) * TOK)
            m = stat[rows, :]
            e0 = jnp.exp2(sbuf[ch, rows, 0:TOK] - m)
            e1 = jnp.exp2(sbuf[ch, rows, TOK:2 * TOK] - m)
            linv[rows, :] += e0 + e1
            ebuf[ch, rows, 0:TOK] = e0.astype(BF16)
            ebuf[ch, rows, TOK:2 * TOK] = e1.astype(BF16)
        return carry

    lax.fori_loop(0, c + 1, exps, 0)
    for h in range(HEADS):
        rows = slice(h * TOK, (h + 1) * TOK)
        inv = 1.0 / jnp.sum(linv[rows, :], axis=1, keepdims=True)
        linv[rows, :] = jnp.broadcast_to(inv, (TOK, HEAD))
        dol[rows, :] = (go[:, rows].astype(F32) * inv).astype(BF16)

    weights = dot_nt(uv[...], dol[...])
    w_hi, w_lo = split2(weights)
    w16 = jnp.concatenate([w_hi, w_lo], axis=0).astype(BF16)

    def lg_copy(to):
        return remote(lgout.at[to], lgin.at[p], ls.at[to], lr.at[p], dev(g, to))

    def grads(i, carry):
        ch = c - i
        both = dot(w16, ebuf[ch])
        lg = GAIN * (both[0:RANK] + both[RANK:2 * RANK])
        lgout[2 * ch] = lg[:, 0:TOK]
        lgout[2 * ch + 1] = lg[:, TOK:2 * TOK]

        @pl.when(2 * ch < p)
        def _():
            lg_copy(2 * ch).start()

        @pl.when(2 * ch + 1 < p)
        def _():
            lg_copy(2 * ch + 1).start()

        return carry

    lax.fori_loop(0, c + 1, grads, 0)

    oacc[...] = jnp.zeros_like(oacc)
    dqacc[...] = jnp.zeros_like(dqacc)

    def outs(i, carry):
        ch = c - i
        v_wait(2 * ch + 1 - yl)
        vc = jnp.concatenate([vbuf[2 * ch, 0:TOK, :], vbuf[2 * ch + 1, 0:TOK, :]], axis=0)
        for h in range(HEADS):
            rows = slice(h * TOK, (h + 1) * TOK)
            oacc[rows, :] += dot(ebuf[ch, rows, :], vc)
            dpbuf[ch, rows, :] = dot_nt(go[:, rows], vc)
        return carry

    lax.fori_loop(0, c + 1, outs, 0)
    for h in range(HEADS):
        rows = slice(h * TOK, (h + 1) * TOK)
        o = oacc[rows, :] * linv[rows, :]
        att[:, rows] = o.astype(BF16)
        center = jnp.sum(o * go[:, rows].astype(F32), axis=1, keepdims=True)
        stat[rows, :] = jnp.broadcast_to(center, (TOK, HEAD))

    unloads = [
        pltpu.make_async_copy(src, dst, unload.at[i])
        for i, (src, dst) in enumerate(((att, att_h), (gdq, gdq_h), (guq, guq_h), (gdv, gdv_h), (guv, guv_h)))
    ]
    unloads[0].start()

    def dquery(i, carry):
        ch = c - i
        kc = keys_of(ch)
        for h in range(HEADS):
            rows = slice(h * TOK, (h + 1) * TOK)
            cen = stat[rows, :]
            d0 = ebuf[ch, rows, 0:TOK].astype(F32) * (dpbuf[ch, rows, 0:TOK] - cen)
            d1 = ebuf[ch, rows, TOK:2 * TOK].astype(F32) * (dpbuf[ch, rows, TOK:2 * TOK] - cen)
            dqacc[rows, :] += dot(jnp.concatenate([d0.astype(BF16), d1.astype(BF16)], axis=1), kc)
        return carry

    lax.fori_loop(0, c + 1, dquery, 0)
    for h in range(HEADS):
        rows = slice(h * TOK, (h + 1) * TOK)
        d_hi, d_lo = split2(dqacc[rows, :] * (linv[rows, :] * ROOT))
        dqhi[:, rows] = d_hi.astype(BF16)
        dqlo[:, rows] = d_lo.astype(BF16)
    lgq = GAIN * (dot_nt(uq[...], dqhi[...]) + dot_nt(uq[...], dqlo[...]))

    def wait_lg(pp, acc):
        arrived(lgin.at[pp], lr.at[pp])
        return acc + lgin[pp]

    lgv = lax.fori_loop(p + 1, group, wait_lg, lgout[p])
    parts2[t] = jnp.concatenate([lgq, lgv], axis=0)

    def part2_copy(i):
        peer = lax.rem(t + i, n_tensor)
        return remote(parts2.at[t], parts2.at[t], p2s.at[i], p2r.at[t], (s, peer))

    def start_part2(i, carry):
        part2_copy(i).start()
        return carry

    lax.fori_loop(1, n_tensor, start_part2, 0)

    lq16 = jnp.concatenate([hi[:RANK], rest[:RANK]], axis=0).astype(BF16)
    g_up = dot(lq16, dqhi[...])
    g_lo = dot(lq16, dqlo[...])
    g_up_q = GAIN * (g_up[:RANK] + g_up[RANK:] + g_lo[:RANK])
    def lows(i, tt):
        ch = c - i
        low16 = jnp.concatenate([vbuf[2 * ch, TOK:TOK + 16, :], vbuf[2 * ch + 1, TOK:TOK + 16, :]], axis=1)
        return tt + dot_nt(low16, ebuf[ch])

    tt = lax.fori_loop(0, c + 1, lows, jnp.zeros((16, HEADS * TOK), F32))
    t_hi, t_lo = split2(tt[:RANK] + tt[RANK:])
    g_v = dot(jnp.concatenate([t_hi, t_lo], axis=0).astype(BF16), dol[...])
    g_up_v = GAIN * (g_v[:RANK] + g_v[RANK:])
    rank_row = lax.broadcasted_iota(jnp.int32, (RANK, HEAD), 0)
    for k in range(chips):
        aout[k, RANK:2 * RANK, :] = g_up_q[:, k * wide:(k + 1) * wide]
        if wide > HEAD:
            aout[k, 3 * RANK:4 * RANK, :] = jnp.zeros((RANK, wide), F32)
        aout[k, 3 * RANK:4 * RANK, 0:HEAD] = jnp.where(lax.rem(rank_row, chips) == k, g_up_v, 0.0)

    def wait_part2(i, carry):
        src = lax.rem(t + i, n_tensor)
        arrived(parts2.at[src], p2r.at[src])
        return carry

    lax.fori_loop(1, n_tensor, wait_part2, 0)
    lowg = parts2[0]
    for i in range(1, n_tensor):
        lowg = lowg + parts2[i]
    g_down = dot(lowg.astype(BF16), hid[...])
    for k in range(chips):
        aout[k, 0:RANK, :] = g_down[0:RANK, k * wide:(k + 1) * wide]
        aout[k, 2 * RANK:3 * RANK, :] = g_down[RANK:2 * RANK, k * wide:(k + 1) * wide]

    def a_copy(i):
        to = lax.rem(c + i, chips)
        return remote(aout.at[to], ain.at[c], asd.at[i], ard.at[c], dev(g, 2 * to + yl))

    def c_copy(i):
        to = lax.rem(c + i, chips)
        return remote(cin.at[c], cin.at[c], csd.at[i], crd.at[c], dev(g, 2 * to + yl))

    mine = 2 * g + yl

    def b_copy(i):
        slot = lax.rem(mine + i, 2 * n_groups)
        return remote(
            bin_.at[mine], bin_.at[mine], bsd.at[i], brd.at[mine],
            dev(slot // 2, 2 * c + lax.rem(slot, 2)),
        )

    def start_a(i, carry):
        a_copy(i).start()
        return carry

    def start_b(i, carry):
        b_copy(i).start()
        return carry

    def start_c(i, carry):
        c_copy(i).start()
        return carry

    def waiter(buf, sem, me, count):
        def body(i, carry):
            src = lax.rem(me + i, count)
            arrived(buf.at[src], sem.at[src])
            return carry

        lax.fori_loop(1, count, body, 0)

    lax.fori_loop(1, chips, start_a, 0)
    ain[c] = aout[c]
    waiter(ain, ard, c, chips)
    total = ain[0]
    for k in range(1, chips):
        total = total + ain[k]
    bin_[mine] = total
    lax.fori_loop(1, 2 * n_groups, start_b, 0)
    waiter(bin_, brd, mine, 2 * n_groups)
    total = bin_[0]
    for k in range(1, 2 * n_groups):
        total = total + bin_[k]
    cin[c] = total
    lax.fori_loop(1, chips, start_c, 0)
    waiter(cin, crd, c, chips)
    up_total = jnp.zeros((RANK, HEAD), F32)
    for k in range(chips):
        gdq[:, k * wide:(k + 1) * wide] = cin[k, 0:RANK, :]
        guq[:, k * wide:(k + 1) * wide] = cin[k, RANK:2 * RANK, :]
        gdv[:, k * wide:(k + 1) * wide] = cin[k, 2 * RANK:3 * RANK, :]
        up_total = up_total + cin[k, 3 * RANK:4 * RANK, 0:HEAD]
    guv[...] = up_total
    for copy in unloads[1:]:
        copy.start()

    def end_tensor(i, carry):
        part1_copy(i).wait_send()
        part2_copy(i).wait_send()
        return carry

    def end_later(to, carry):
        k_copy(to).wait_send()
        v_copy(to).wait_send()
        return carry

    def end_pair(frm, carry):
        k_pair(frm).wait_send()
        v_pair(frm).wait_send()
        return carry

    def end_lg(to, carry):
        lg_copy(to).wait_send()
        return carry

    def end_row(i, carry):
        a_copy(i).wait_send()
        c_copy(i).wait_send()
        return carry

    def end_far(i, carry):
        b_copy(i).wait_send()
        return carry

    lax.fori_loop(1, n_tensor, end_tensor, 0)
    lax.fori_loop(c + 1, chips, end_later, 0)
    lax.fori_loop(0, c + 1, end_pair, 0)
    lax.fori_loop(0, p, end_lg, 0)
    lax.fori_loop(1, chips, end_row, 0)
    lax.fori_loop(1, 2 * n_groups, end_far, 0)
    for copy in unloads:
        copy.wait()


def store(*refs):
    made, out, held, sem = refs[0:5], refs[5:10], refs[10:15], refs[15]
    copies = [pltpu.make_async_copy(made[i], held[i], sem.at[0, i]) for i in range(5)]
    backs = [pltpu.make_async_copy(held[i], out[i], sem.at[1, i]) for i in range(5)]
    for copy in copies:
        copy.start()
    for copy, back in zip(copies, backs):
        copy.wait()
        back.start()
    for back in backs:
        back.wait()


def solution(mesh, group_tokens=GROUP_TOKENS):
    n_seq, n_tensor = mesh.shape["seq"], mesh.shape["tensor"]
    group = group_tokens // TOK
    chips = group // 2
    far = 2 * (n_seq // group)
    wide = WIDTH // chips
    rows = HEADS * TOK
    dma = pltpu.SemaphoreType.DMA

    hbm = pl.BlockSpec(memory_space=pltpu.HBM)
    results = (
        jax.ShapeDtypeStruct((TOK, WIDTH), BF16),
        jax.ShapeDtypeStruct((RANK, WIDTH), F32),
        jax.ShapeDtypeStruct((RANK, WIDTH), F32),
        jax.ShapeDtypeStruct((RANK, WIDTH), F32),
        jax.ShapeDtypeStruct((RANK, HEAD), F32),
    )

    def per_device(*args):
        made = pl.pallas_call(
            functools.partial(kernel, n_seq, n_tensor, group),
            out_shape=results,
            in_specs=[hbm] * 9,
            out_specs=(hbm,) * 5,
            scratch_shapes=[pltpu.VMEM(a.shape, a.dtype) for a in results] + [dma((5,))]
            + [pltpu.VMEM(a.shape, a.dtype) for a in args] + [
                dma((9,)),
                pltpu.VMEM((n_tensor, 2 * RANK, TOK), F32),
                pltpu.VMEM((n_tensor, 2 * RANK, TOK), F32),
                pltpu.VMEM((group, TOK, HEAD), BF16),
                pltpu.VMEM((group, TOK + 16, HEAD), BF16),
                pltpu.VMEM((TOK + 16, HEAD), BF16),
                pltpu.VMEM((group, RANK, TOK), F32),
                pltpu.VMEM((group, RANK, TOK), F32),
                pltpu.VMEM((chips, 4 * RANK, wide), F32),
                pltpu.VMEM((far, 4 * RANK, wide), F32),
                pltpu.VMEM((chips, 4 * RANK, wide), F32),
                pltpu.VMEM((chips, 4 * RANK, wide), F32),
                pltpu.VMEM((rows, HEAD), BF16),
                pltpu.VMEM((chips, rows, 2 * TOK), F32),
                pltpu.VMEM((chips, rows, 2 * TOK), BF16),
                pltpu.VMEM((chips, rows, 2 * TOK), F32),
                pltpu.VMEM((rows, HEAD), F32),
                pltpu.VMEM((rows, HEAD), F32),
                pltpu.VMEM((rows, HEAD), F32),
                pltpu.VMEM((rows, HEAD), F32),
                pltpu.VMEM((rows, HEAD), BF16),
                pltpu.VMEM((TOK, WIDTH), BF16),
                pltpu.VMEM((TOK, WIDTH), BF16),
                dma((n_tensor,)), dma((n_tensor,)),
                dma((chips,)), dma((chips,)), dma((group,)),
                dma((chips,)), dma((chips,)), dma((group,)),
                dma((group,)), dma((group,)),
                dma((n_tensor,)), dma((n_tensor,)),
                dma((chips,)), dma((chips,)),
                dma((far,)), dma((far,)),
                dma((chips,)), dma((chips,)),
            ],
            compiler_params=pltpu.CompilerParams(
                collective_id=0, has_side_effects=True, vmem_limit_bytes=60 * 1024 * 1024
            ),
        )(*args)
        return pl.pallas_call(
            store,
            out_shape=results,
            in_specs=[hbm] * 5,
            out_specs=(hbm,) * 5,
            scratch_shapes=[pltpu.VMEM(a.shape, a.dtype) for a in results] + [dma((2, 5))],
            compiler_params=pltpu.CompilerParams(vmem_limit_bytes=60 * 1024 * 1024),
        )(*made)

    split = P("seq", "tensor")
    cols = P(None, "tensor")
    return jax.shard_map(
        per_device,
        mesh=mesh,
        in_specs=(split, split, split, split, cols, cols, cols, cols, split),
        out_specs=(split, cols, cols, cols, cols),
        check_vma=False,
    )
```

```python
import functools
import math

import jax
import jax.numpy as jnp
from jax import lax
from jax.experimental import pallas as pl
from jax.experimental.pallas import tpu as pltpu
from jax.sharding import PartitionSpec as P

MESH = pl.DeviceIdType.MESH
GROUP_TOKENS = 2048
HEADS = 8
HEAD = 128
RANK = 8
TOK = 128
WIDTH = HEADS * HEAD
GAIN = 2.0
ROOT = HEAD ** -0.5
LOG2E = math.log2(math.e)
F32 = jnp.float32
BF16 = jnp.bfloat16
NT = (((1,), (1,)), ((), ()))


def paced(count, body, width):
    def step(i, carry):
        for j in range(width):
            body(i * width + j)
        return carry

    def rest(i, carry):
        body(i)
        return carry

    whole = count // width
    lax.fori_loop(0, whole, step, 0)
    lax.fori_loop(whole * width, count, rest, 0)


def dot(a, b):
    return jnp.dot(a, b, preferred_element_type=F32)


def dot_nt(a, b):
    return lax.dot_general(a, b, NT, preferred_element_type=F32)


def split2(x):
    hi = x.astype(BF16).astype(F32)
    return hi, x - hi


def arrived(buf, sem):
    pltpu.make_async_copy(buf, buf, sem).wait()


def kernel(
    n_seq, n_tensor, group,
    hid_h, qb_h, kp_h, fv_h, dq_h, uq_h, dv_h, uv_h, go_h,
    att_h, gdq_h, guq_h, gdv_h, guv_h,
    att, gdq, guq, gdv, guv, unload,
    hid, qb, kp, fv, dq, uq, dv, uv, go, load,
    parts1, parts2, kbuf, vbuf, vown, lgout, lgin, ain, bin_, cin, aout,
    qs, sbuf, ebuf, dpbuf, stat, linv, oacc, dqacc, dol, dqhi, dqlo,
    p1s, p1r, ks, kf, kr, vs, vf, vr, ls, lr, p2s, p2r, asd, ard, bsd, brd, csd, crd,
):
    s = lax.axis_index("seq")
    t = lax.axis_index("tensor")
    chips = group // 2
    n_groups = n_seq // group
    wide = WIDTH // chips
    lag = jnp.where(t >= n_tensor // 2, group // 2, 0)
    rolled = lax.rem(s - lag + n_seq, n_seq)
    g = rolled // group
    p = lax.rem(rolled, group)
    c = p // 2
    yl = lax.rem(p, 2)
    mate = 2 * c + 1 - yl

    def place(gg, pp):
        return lax.rem(gg * group + pp + lag, n_seq)

    def dev(gg, pp):
        return (place(gg, pp), t)

    def remote(src, dst, send, recv, device):
        return pltpu.make_async_remote_copy(
            src_ref=src, dst_ref=dst, send_sem=send, recv_sem=recv,
            device_id=device, device_id_type=MESH,
        )

    loads = [
        pltpu.make_async_copy(src, dst, load.at[i])
        for i, (src, dst) in enumerate((
            (kp_h, kp), (hid_h, hid), (dq_h, dq), (dv_h, dv), (fv_h, fv), (uv_h, uv), (uq_h, uq), (qb_h, qb), (go_h, go),
        ))
    ]
    for copy in loads[:4]:
        copy.start()

    barrier = pltpu.get_barrier_semaphore()

    def greet(device):
        pl.semaphore_signal(barrier, inc=1, device_id=device, device_id_type=MESH)

    def greet_tensor(i, carry):
        greet((s, lax.rem(t + i, n_tensor)))
        return carry

    def greet_group(i, carry):
        greet(dev(g, lax.rem(p + i, group)))
        return carry

    def greet_far(i, carry):
        greet(dev(lax.rem(g + 1 + i // 2, n_groups), 2 * c + lax.rem(i, 2)))
        return carry

    lax.fori_loop(1, n_tensor, greet_tensor, 0)
    lax.fori_loop(1, group, greet_group, 0)
    lax.fori_loop(0, 2 * (n_groups - 1), greet_far, 0)

    for copy in loads[4:]:
        copy.start()
    loads[0].wait()
    kbuf[p] = kp[...]
    pl.semaphore_wait(barrier, (n_tensor - 1) + (group - 1) + 2 * (n_groups - 1))

    def part1_copy(i):
        peer = lax.rem(t + i, n_tensor)
        return remote(parts1.at[t], parts1.at[t], p1s.at[i], p1r.at[t], (s, peer))

    def start_part1(i, carry):
        part1_copy(i).start()
        return carry


    def k_copy(to):
        return remote(kp, kbuf.at[p], ks.at[to], kr.at[p], dev(g, 2 * to + yl))

    def k_pair(frm):
        return remote(kbuf.at[2 * frm + yl], kbuf.at[2 * frm + yl], kf.at[frm], kr.at[2 * frm + yl], dev(g, mate))

    def v_copy(to):
        return remote(vown, vbuf.at[p], vs.at[to], vr.at[p], dev(g, 2 * to + yl))

    def v_pair(frm):
        return remote(vbuf.at[2 * frm + yl], vbuf.at[2 * frm + yl], vf.at[frm], vr.at[2 * frm + yl], dev(g, mate))

    def k_wait(pp):
        arrived(kbuf.at[pp], kr.at[pp])

    def v_wait(pp):
        arrived(vbuf.at[pp], vr.at[pp])

    def start_k(to, carry):
        k_copy(to).start()
        return carry

    lax.fori_loop(c + 1, chips, start_k, 0)

    for copy in loads[1:4]:
        copy.wait()
    down = jnp.concatenate([dq[...].astype(F32), dv[...].astype(F32)], axis=0).astype(BF16)
    parts1[t] = dot_nt(down, hid[...])
    lax.fori_loop(1, n_tensor, start_part1, 0)
    k_pair(c).start()

    for copy in loads[4:]:
        copy.wait()

    def forward_k(i, carry):
        frm = c - 1 - i
        k_wait(2 * frm + yl)
        k_pair(frm).start()
        return carry

    lax.fori_loop(0, c, forward_k, 0)

    def wait_part1(i, carry):
        src = lax.rem(t + i, n_tensor)
        arrived(parts1.at[src], p1r.at[src])
        return carry

    lax.fori_loop(1, n_tensor, wait_part1, 0)
    low = parts1[0]
    for i in range(1, n_tensor):
        low = low + parts1[i]
    hi = low.astype(BF16).astype(F32)
    rest = low - hi
    mid = rest.astype(BF16).astype(F32)
    lo = rest - mid
    zeros = jnp.zeros((TOK - 48, TOK), F32)
    pieces = jnp.transpose(jnp.concatenate([hi, mid, lo, zeros], axis=0)).astype(BF16)
    none_q = jnp.zeros((RANK, WIDTH), F32)
    none_v = jnp.zeros((RANK, HEAD), F32)
    uqf = uq[...].astype(F32)
    uvf = uv[...].astype(F32)
    up_v = jnp.concatenate([none_v, uvf] * 3 + [jnp.zeros((TOK - 48, HEAD), F32)], axis=0).astype(BF16)
    value = (fv[...].astype(F32) + GAIN * dot(pieces, up_v)).astype(BF16)
    low_v = jnp.concatenate([hi[RANK:], rest[RANK:]], axis=0).astype(BF16)
    vown[0:TOK, :] = value
    vown[TOK:TOK + 16, :] = low_v
    vbuf[p] = vown[...]

    v_pair(c).start()

    def start_v(to, carry):
        v_copy(to).start()
        return carry

    lax.fori_loop(c + 1, chips, start_v, 0)

    up_q = jnp.concatenate([uqf, none_q] * 3 + [jnp.zeros((TOK - 48, WIDTH), F32)], axis=0).astype(BF16)
    for h in range(HEADS):
        cols = slice(h * HEAD, (h + 1) * HEAD)
        qs[cols, :] = (qb[:, cols].astype(F32) + GAIN * dot(pieces, up_q[:, cols])).astype(BF16)

    def keys_of(ch):
        return kbuf[pl.ds(2 * ch, 2)].reshape(2 * TOK, HEAD)

    k_wait(mate)
    kc = keys_of(c)
    column = lax.broadcasted_iota(jnp.int32, (TOK, 2 * TOK), 1)
    row = lax.broadcasted_iota(jnp.int32, (TOK, 2 * TOK), 0)
    allowed = column <= row + yl * TOK
    for h in range(HEADS):
        rows = slice(h * TOK, (h + 1) * TOK)
        sc = jnp.where(allowed, dot_nt(qs[rows, :], kc) * (ROOT * LOG2E), -1e30)
        sbuf[c, rows, :] = sc
        stat[rows, :] = jnp.maximum(sc[:, :TOK], sc[:, TOK:])

    def forward_v(i):
        frm = c - 1 - i
        v_wait(2 * frm + yl)
        v_pair(frm).start()

    def scores(i):
        ch = c - 1 - i

        k_wait(2 * ch + 1 - yl)
        kc = keys_of(ch)
        for h in range(HEADS):
            rows = slice(h * TOK, (h + 1) * TOK)
            sc = dot_nt(qs[rows, :], kc) * (ROOT * LOG2E)
            sbuf[ch, rows, :] = sc
            stat[rows, :] = jnp.maximum(stat[rows, :], jnp.maximum(sc[:, :TOK], sc[:, TOK:]))

    paced(c, scores, 2)
    for h in range(HEADS):
        rows = slice(h * TOK, (h + 1) * TOK)
        stat[rows, :] = jnp.broadcast_to(jnp.max(stat[rows, :], axis=1, keepdims=True), (TOK, HEAD))
    linv[...] = jnp.zeros_like(linv)

    def exps(i):
        ch = c - i
        ahead = i - 1

        @pl.when(i > 0)
        def _():
            forward_v(ahead)

        for h in range(HEADS):
            rows = slice(h * TOK, (h + 1) * TOK)
            m = stat[rows, :]
            e0 = jnp.exp2(sbuf[ch, rows, 0:TOK] - m)
            e1 = jnp.exp2(sbuf[ch, rows, TOK:2 * TOK] - m)
            linv[rows, :] += e0 + e1
            ebuf[ch, rows, 0:TOK] = e0.astype(BF16)
            ebuf[ch, rows, TOK:2 * TOK] = e1.astype(BF16)

    paced(c + 1, exps, 2)
    for h in range(HEADS):
        rows = slice(h * TOK, (h + 1) * TOK)
        inv = 1.0 / jnp.sum(linv[rows, :], axis=1, keepdims=True)
        linv[rows, :] = jnp.broadcast_to(inv, (TOK, HEAD))
        dol[rows, :] = (go[:, rows].astype(F32) * inv).astype(BF16)

    weights = dot_nt(uv[...], dol[...])
    w_hi, w_lo = split2(weights)
    w16 = jnp.concatenate([w_hi, w_lo], axis=0).astype(BF16)

    def lg_copy(to):
        return remote(lgout.at[to], lgin.at[p], ls.at[to], lr.at[p], dev(g, to))

    def grads(i):
        ch = c - i
        both = dot(w16, ebuf[ch])
        lg = GAIN * (both[0:RANK] + both[RANK:2 * RANK])
        lgout[2 * ch] = lg[:, 0:TOK]
        lgout[2 * ch + 1] = lg[:, TOK:2 * TOK]

        @pl.when(2 * ch < p)
        def _():
            lg_copy(2 * ch).start()

        @pl.when(2 * ch + 1 < p)
        def _():
            lg_copy(2 * ch + 1).start()

    paced(c + 1, grads, 2)

    oacc[...] = jnp.zeros_like(oacc)
    dqacc[...] = jnp.zeros_like(dqacc)

    def outs(i):
        ch = c - i
        v_wait(2 * ch + 1 - yl)

        vc = jnp.concatenate([vbuf[2 * ch, 0:TOK, :], vbuf[2 * ch + 1, 0:TOK, :]], axis=0)
        for h in range(HEADS):
            rows = slice(h * TOK, (h + 1) * TOK)
            oacc[rows, :] += dot(ebuf[ch, rows, :], vc)
            dpbuf[ch, rows, :] = dot_nt(go[:, rows], vc)

    paced(c + 1, outs, 2)
    for h in range(HEADS):
        rows = slice(h * TOK, (h + 1) * TOK)
        o = oacc[rows, :] * linv[rows, :]
        att[:, rows] = o.astype(BF16)
        center = jnp.sum(o * go[:, rows].astype(F32), axis=1, keepdims=True)
        stat[rows, :] = jnp.broadcast_to(center, (TOK, HEAD))

    unloads = [
        pltpu.make_async_copy(src, dst, unload.at[i])
        for i, (src, dst) in enumerate(((att, att_h), (gdq, gdq_h), (guq, guq_h), (gdv, gdv_h), (guv, guv_h)))
    ]
    unloads[0].start()

    def dquery(first, width):
        kc = kbuf[pl.ds(2 * first, 2 * width)].reshape(2 * width * TOK, HEAD)
        for h in range(HEADS):
            rows = slice(h * TOK, (h + 1) * TOK)
            cen = stat[rows, :]
            ds = []
            for j in range(width):
                for half in (slice(0, TOK), slice(TOK, 2 * TOK)):
                    part = dpbuf[first + j, rows, half] - cen
                    ds.append((ebuf[first + j, rows, half].astype(F32) * part).astype(BF16))
            dqacc[rows, :] += dot(jnp.concatenate(ds, axis=1), kc)

    def dquery_four(i, carry):
        dquery(4 * i, 4)
        return carry

    def dquery_one(i, carry):
        dquery(i, 1)
        return carry

    fours = (c + 1) // 4
    lax.fori_loop(0, fours, dquery_four, 0)
    lax.fori_loop(4 * fours, c + 1, dquery_one, 0)
    for h in range(HEADS):
        rows = slice(h * TOK, (h + 1) * TOK)
        d_hi, d_lo = split2(dqacc[rows, :] * (linv[rows, :] * ROOT))
        dqhi[:, rows] = d_hi.astype(BF16)
        dqlo[:, rows] = d_lo.astype(BF16)
    lgq = GAIN * (dot_nt(uq[...], dqhi[...]) + dot_nt(uq[...], dqlo[...]))

    def wait_lg(pp, acc):
        arrived(lgin.at[pp], lr.at[pp])
        return acc + lgin[pp]

    lgv = lax.fori_loop(p + 1, group, wait_lg, lgout[p])
    parts2[t] = jnp.concatenate([lgq, lgv], axis=0)

    def part2_copy(i):
        peer = lax.rem(t + i, n_tensor)
        return remote(parts2.at[t], parts2.at[t], p2s.at[i], p2r.at[t], (s, peer))

    def start_part2(i, carry):
        part2_copy(i).start()
        return carry

    lax.fori_loop(1, n_tensor, start_part2, 0)

    lq16 = jnp.concatenate([hi[:RANK], rest[:RANK]], axis=0).astype(BF16)
    g_up = dot(lq16, dqhi[...])
    g_lo = dot(lq16, dqlo[...])
    g_up_q = GAIN * (g_up[:RANK] + g_up[RANK:] + g_lo[:RANK])
    def lows(i, tt):
        ch = c - i
        low16 = jnp.concatenate([vbuf[2 * ch, TOK:TOK + 16, :], vbuf[2 * ch + 1, TOK:TOK + 16, :]], axis=1)
        return tt + dot_nt(low16, ebuf[ch])

    tt = lax.fori_loop(0, c + 1, lows, jnp.zeros((16, HEADS * TOK), F32))
    t_hi, t_lo = split2(tt[:RANK] + tt[RANK:])
    g_v = dot(jnp.concatenate([t_hi, t_lo], axis=0).astype(BF16), dol[...])
    g_up_v = GAIN * (g_v[:RANK] + g_v[RANK:])
    rank_row = lax.broadcasted_iota(jnp.int32, (RANK, HEAD), 0)
    for k in range(chips):
        aout[k, RANK:2 * RANK, :] = g_up_q[:, k * wide:(k + 1) * wide]
        if wide > HEAD:
            aout[k, 3 * RANK:4 * RANK, :] = jnp.zeros((RANK, wide), F32)
        aout[k, 3 * RANK:4 * RANK, 0:HEAD] = jnp.where(lax.rem(rank_row, chips) == k, g_up_v, 0.0)

    def end_tensor(i, carry):
        part1_copy(i).wait_send()
        return carry

    def end_row(to, carry):
        k_copy(to).wait_send()
        v_copy(to).wait_send()
        return carry

    def end_pair(frm, carry):
        k_pair(frm).wait_send()
        v_pair(frm).wait_send()
        return carry

    def end_lg(to, carry):
        lg_copy(to).wait_send()
        return carry

    lax.fori_loop(1, n_tensor, end_tensor, 0)
    lax.fori_loop(c + 1, chips, end_row, 0)
    lax.fori_loop(0, c + 1, end_pair, 0)
    lax.fori_loop(0, p, end_lg, 0)

    def wait_part2(i, carry):
        src = lax.rem(t + i, n_tensor)
        arrived(parts2.at[src], p2r.at[src])
        return carry

    lax.fori_loop(1, n_tensor, wait_part2, 0)
    lowg = parts2[0]
    for i in range(1, n_tensor):
        lowg = lowg + parts2[i]
    g_down = dot(lowg.astype(BF16), hid[...])
    for k in range(chips):
        aout[k, 0:RANK, :] = g_down[0:RANK, k * wide:(k + 1) * wide]
        aout[k, 2 * RANK:3 * RANK, :] = g_down[RANK:2 * RANK, k * wide:(k + 1) * wide]

    def a_copy(i):
        to = lax.rem(c + i, chips)
        return remote(aout.at[to], ain.at[c], asd.at[i], ard.at[c], dev(g, 2 * to + yl))

    def c_copy(i):
        to = lax.rem(c + i, chips)
        return remote(cin.at[c], cin.at[c], csd.at[i], crd.at[c], dev(g, 2 * to + yl))

    mine = 2 * g + yl

    def b_copy(i):
        slot = lax.rem(mine + i, 2 * n_groups)
        return remote(
            bin_.at[mine], bin_.at[mine], bsd.at[i], brd.at[mine],
            dev(slot // 2, 2 * c + lax.rem(slot, 2)),
        )

    def start_a(i, carry):
        a_copy(i).start()
        return carry

    def start_b(i, carry):
        b_copy(i).start()
        return carry

    def start_c(i, carry):
        c_copy(i).start()
        return carry

    def waiter(buf, sem, me, count):
        def body(i, carry):
            src = lax.rem(me + i, count)
            arrived(buf.at[src], sem.at[src])
            return carry

        lax.fori_loop(1, count, body, 0)

    lax.fori_loop(1, chips, start_a, 0)
    ain[c] = aout[c]
    waiter(ain, ard, c, chips)
    total = ain[0]
    for k in range(1, chips):
        total = total + ain[k]
    bin_[mine] = total
    lax.fori_loop(1, 2 * n_groups, start_b, 0)
    waiter(bin_, brd, mine, 2 * n_groups)
    total = bin_[0]
    for k in range(1, 2 * n_groups):
        total = total + bin_[k]
    cin[c] = total
    lax.fori_loop(1, chips, start_c, 0)

    def end_tensor2(i, carry):
        part2_copy(i).wait_send()
        return carry

    def end_a(i, carry):
        a_copy(i).wait_send()
        return carry

    def end_b(i, carry):
        b_copy(i).wait_send()
        return carry

    def end_c(i, carry):
        c_copy(i).wait_send()
        return carry

    lax.fori_loop(1, n_tensor, end_tensor2, 0)
    lax.fori_loop(1, chips, end_a, 0)
    lax.fori_loop(1, 2 * n_groups, end_b, 0)
    waiter(cin, crd, c, chips)
    up_total = jnp.zeros((RANK, HEAD), F32)
    for k in range(chips):
        gdq[:, k * wide:(k + 1) * wide] = cin[k, 0:RANK, :]
        guq[:, k * wide:(k + 1) * wide] = cin[k, RANK:2 * RANK, :]
        gdv[:, k * wide:(k + 1) * wide] = cin[k, 2 * RANK:3 * RANK, :]
        up_total = up_total + cin[k, 3 * RANK:4 * RANK, 0:HEAD]
    guv[...] = up_total
    for copy in unloads[1:]:
        copy.start()
    lax.fori_loop(1, chips, end_c, 0)

    for copy in unloads:
        copy.wait()


def store(*refs):
    made, out, held, sem = refs[0:5], refs[5:10], refs[10:15], refs[15]
    copies = [pltpu.make_async_copy(made[i], held[i], sem.at[0, i]) for i in range(5)]
    backs = [pltpu.make_async_copy(held[i], out[i], sem.at[1, i]) for i in range(5)]
    for copy in copies:
        copy.start()
    for copy, back in zip(copies, backs):
        copy.wait()
        back.start()
    for back in backs:
        back.wait()


def solution(mesh, group_tokens=GROUP_TOKENS):
    n_seq, n_tensor = mesh.shape["seq"], mesh.shape["tensor"]
    group = group_tokens // TOK
    chips = group // 2
    far = 2 * (n_seq // group)
    wide = WIDTH // chips
    rows = HEADS * TOK
    dma = pltpu.SemaphoreType.DMA

    hbm = pl.BlockSpec(memory_space=pltpu.HBM)
    results = (
        jax.ShapeDtypeStruct((TOK, WIDTH), BF16),
        jax.ShapeDtypeStruct((RANK, WIDTH), F32),
        jax.ShapeDtypeStruct((RANK, WIDTH), F32),
        jax.ShapeDtypeStruct((RANK, WIDTH), F32),
        jax.ShapeDtypeStruct((RANK, HEAD), F32),
    )

    def per_device(*args):
        made = pl.pallas_call(
            functools.partial(kernel, n_seq, n_tensor, group),
            out_shape=results,
            in_specs=[hbm] * 9,
            out_specs=(hbm,) * 5,
            scratch_shapes=[pltpu.VMEM(a.shape, a.dtype) for a in results] + [dma((5,))]
            + [pltpu.VMEM(a.shape, a.dtype) for a in args] + [
                dma((9,)),
                pltpu.VMEM((n_tensor, 2 * RANK, TOK), F32),
                pltpu.VMEM((n_tensor, 2 * RANK, TOK), F32),
                pltpu.VMEM((group, TOK, HEAD), BF16),
                pltpu.VMEM((group, TOK + 16, HEAD), BF16),
                pltpu.VMEM((TOK + 16, HEAD), BF16),
                pltpu.VMEM((group, RANK, TOK), F32),
                pltpu.VMEM((group, RANK, TOK), F32),
                pltpu.VMEM((chips, 4 * RANK, wide), F32),
                pltpu.VMEM((far, 4 * RANK, wide), F32),
                pltpu.VMEM((chips, 4 * RANK, wide), F32),
                pltpu.VMEM((chips, 4 * RANK, wide), F32),
                pltpu.VMEM((rows, HEAD), BF16),
                pltpu.VMEM((chips, rows, 2 * TOK), F32),
                pltpu.VMEM((chips, rows, 2 * TOK), BF16),
                pltpu.VMEM((chips, rows, 2 * TOK), F32),
                pltpu.VMEM((rows, HEAD), F32),
                pltpu.VMEM((rows, HEAD), F32),
                pltpu.VMEM((rows, HEAD), F32),
                pltpu.VMEM((rows, HEAD), F32),
                pltpu.VMEM((rows, HEAD), BF16),
                pltpu.VMEM((TOK, WIDTH), BF16),
                pltpu.VMEM((TOK, WIDTH), BF16),
                dma((n_tensor,)), dma((n_tensor,)),
                dma((chips,)), dma((chips,)), dma((group,)),
                dma((chips,)), dma((chips,)), dma((group,)),
                dma((group,)), dma((group,)),
                dma((n_tensor,)), dma((n_tensor,)),
                dma((chips,)), dma((chips,)),
                dma((far,)), dma((far,)),
                dma((chips,)), dma((chips,)),
            ],
            compiler_params=pltpu.CompilerParams(
                collective_id=0, has_side_effects=True, vmem_limit_bytes=60 * 1024 * 1024
            ),
        )(*args)
        return pl.pallas_call(
            store,
            out_shape=results,
            in_specs=[hbm] * 5,
            out_specs=(hbm,) * 5,
            scratch_shapes=[pltpu.VMEM(a.shape, a.dtype) for a in results] + [dma((2, 5))],
            compiler_params=pltpu.CompilerParams(vmem_limit_bytes=60 * 1024 * 1024),
        )(*made)

    split = P("seq", "tensor")
    cols = P(None, "tensor")
    return jax.shard_map(
        per_device,
        mesh=mesh,
        in_specs=(split, split, split, split, cols, cols, cols, cols, split),
        out_specs=(split, cols, cols, cols, cols),
        check_vma=False,
    )
```

```python
import functools
import math

import jax
import jax.numpy as jnp
from jax import lax
from jax.experimental import pallas as pl
from jax.experimental.pallas import tpu as pltpu
from jax.sharding import PartitionSpec as P

MESH = pl.DeviceIdType.MESH
GROUP_TOKENS = 2048
HEADS = 8
HEAD = 128
RANK = 8
TOK = 128
WIDTH = HEADS * HEAD
GAIN = 2.0
ROOT = HEAD ** -0.5
LOG2E = math.log2(math.e)
F32 = jnp.float32
BF16 = jnp.bfloat16
NT = (((1,), (1,)), ((), ()))


def paced(count, body, width):
    def step(i, carry):
        for j in range(width):
            body(i * width + j)
        return carry

    def rest(i, carry):
        body(i)
        return carry

    whole = count // width
    lax.fori_loop(0, whole, step, 0)
    lax.fori_loop(whole * width, count, rest, 0)


def arrived_all(buf, sem, count):
    if count > 1:
        arrived(buf.at[pl.ds(0, count - 1)], sem.at[0])


def dot(a, b):
    return jnp.dot(a, b, preferred_element_type=F32)


def dot_nt(a, b):
    return lax.dot_general(a, b, NT, preferred_element_type=F32)


def split2(x):
    hi = x.astype(BF16).astype(F32)
    return hi, x - hi


def arrived(buf, sem):
    pltpu.make_async_copy(buf, buf, sem).wait()


def kernel(
    n_seq, n_tensor, group,
    hid_h, qb_h, kp_h, fv_h, dq_h, uq_h, dv_h, uv_h, go_h,
    att_h, gdq_h, guq_h, gdv_h, guv_h,
    att, gdq, guq, gdv, guv, unload,
    hid, qb, kp, fv, dq, uq, dv, uv, go, load,
    parts1, parts2, kbuf, vbuf, vown, lgout, lgin, ain, bin_, cin, aout,
    qs, sbuf, ebuf, dpbuf, stat, linv, oacc, dqacc, dol, dqhi, dqlo,
    p1s, p1r, ks, kf, kr, vs, vr, ls, lr, p2s, p2r, asd, ard, bsd, brd, csd, crd,
):
    s = lax.axis_index("seq")
    t = lax.axis_index("tensor")
    chips = group // 2
    n_groups = n_seq // group
    wide = WIDTH // chips
    lag = jnp.where(t >= n_tensor // 2, group // 2, 0)
    rolled = lax.rem(s - lag + n_seq, n_seq)
    g = rolled // group
    p = lax.rem(rolled, group)
    c = p // 2
    yl = lax.rem(p, 2)
    mate = 2 * c + 1 - yl

    def place(gg, pp):
        return lax.rem(gg * group + pp + lag, n_seq)

    def dev(gg, pp):
        return (place(gg, pp), t)

    def remote(src, dst, send, recv, device):
        return pltpu.make_async_remote_copy(
            src_ref=src, dst_ref=dst, send_sem=send, recv_sem=recv,
            device_id=device, device_id_type=MESH,
        )

    loads = [
        pltpu.make_async_copy(src, dst, load.at[i])
        for i, (src, dst) in enumerate((
            (kp_h, kp), (hid_h, hid), (dq_h, dq), (dv_h, dv), (fv_h, fv), (uv_h, uv), (uq_h, uq), (qb_h, qb), (go_h, go),
        ))
    ]
    for copy in loads[:4]:
        copy.start()

    barrier = pltpu.get_barrier_semaphore()

    def greet(device):
        pl.semaphore_signal(barrier, inc=1, device_id=device, device_id_type=MESH)

    def greet_tensor(i, carry):
        greet((s, lax.rem(t + i, n_tensor)))
        return carry

    def greet_group(i, carry):
        greet(dev(g, lax.rem(p + i, group)))
        return carry

    def greet_far(i, carry):
        greet(dev(lax.rem(g + 1 + i // 2, n_groups), 2 * c + lax.rem(i, 2)))
        return carry

    lax.fori_loop(1, n_tensor, greet_tensor, 0)
    lax.fori_loop(1, group, greet_group, 0)
    lax.fori_loop(0, 2 * (n_groups - 1), greet_far, 0)

    for copy in loads[4:]:
        copy.start()
    loads[0].wait()
    kbuf[p] = kp[...]

    for copy in loads[1:4]:
        copy.wait()
    down = jnp.concatenate([dq[...].astype(F32), dv[...].astype(F32)], axis=0).astype(BF16)
    parts1[t] = dot_nt(down, hid[...])
    pl.semaphore_wait(barrier, (n_tensor - 1) + (group - 1) + 2 * (n_groups - 1))

    def part1_copy(i):
        peer = lax.rem(t + i, n_tensor)
        return remote(parts1.at[t], parts1.at[t], p1s.at[0], p1r.at[0], (s, peer))

    def start_part1(i, carry):
        part1_copy(i).start()
        return carry


    def k_copy(to):
        return remote(kp, kbuf.at[p], ks.at[to], kr.at[p], dev(g, 2 * to + yl))

    def k_pair(frm):
        return remote(kbuf.at[2 * frm + yl], kbuf.at[2 * frm + yl], kf.at[frm], kr.at[2 * frm + yl], dev(g, mate))

    def v_copy(to):
        return remote(vown, vbuf.at[p], vs.at[to], vr.at[p], dev(g, to))

    def k_wait(pp):
        arrived(kbuf.at[pp], kr.at[pp])

    def v_wait(pp):
        arrived(vbuf.at[pp], vr.at[pp])

    lax.fori_loop(1, n_tensor, start_part1, 0)
    def start_k(to, carry):
        k_copy(to).start()
        return carry

    lax.fori_loop(c + 1, chips, start_k, 0)
    k_pair(c).start()

    for copy in loads[4:]:
        copy.wait()

    def forward_k(i, carry):
        frm = c - 1 - i
        k_wait(2 * frm + yl)
        k_pair(frm).start()
        return carry

    lax.fori_loop(0, c, forward_k, 0)

    none_q = jnp.zeros((RANK, WIDTH), F32)
    none_v = jnp.zeros((RANK, HEAD), F32)
    uqf = uq[...].astype(F32)
    uvf = uv[...].astype(F32)
    up_v = jnp.concatenate([none_v, uvf] * 3 + [jnp.zeros((TOK - 48, HEAD), F32)], axis=0).astype(BF16)
    up_q = jnp.concatenate([uqf, none_q] * 3 + [jnp.zeros((TOK - 48, WIDTH), F32)], axis=0).astype(BF16)

    arrived_all(parts1, p1r, n_tensor)
    low = parts1[0]
    for i in range(1, n_tensor):
        low = low + parts1[i]
    hi = low.astype(BF16).astype(F32)
    rest = low - hi
    mid = rest.astype(BF16).astype(F32)
    lo = rest - mid
    zeros = jnp.zeros((TOK - 48, TOK), F32)
    pieces = jnp.transpose(jnp.concatenate([hi, mid, lo, zeros], axis=0)).astype(BF16)
    value = (fv[...].astype(F32) + GAIN * dot(pieces, up_v)).astype(BF16)
    low_v = jnp.concatenate([hi[RANK:], rest[RANK:]], axis=0).astype(BF16)
    vown[0:TOK, :] = value
    vown[TOK:TOK + 16, :] = low_v
    vbuf[p] = vown[...]

    @pl.when(yl == 0)
    def _():
        vbuf[mate] = jnp.zeros((TOK + 16, HEAD), BF16)


    def start_v(to, carry):
        v_copy(to).start()
        return carry

    lax.fori_loop(c + yl, chips, lambda i, q: start_v(2 * i + 1 - yl, q), 0)
    lax.fori_loop(c + 1, chips, lambda i, q: start_v(2 * i + yl, q), 0)

    for h in range(HEADS):
        cols = slice(h * HEAD, (h + 1) * HEAD)
        qs[cols, :] = (qb[:, cols].astype(F32) + GAIN * dot(pieces, up_q[:, cols])).astype(BF16)

    def keys_of(ch):
        return kbuf[pl.ds(2 * ch, 2)].reshape(2 * TOK, HEAD)

    k_wait(mate)
    kc = keys_of(c)
    column = lax.broadcasted_iota(jnp.int32, (TOK, 2 * TOK), 1)
    row = lax.broadcasted_iota(jnp.int32, (TOK, 2 * TOK), 0)
    allowed = column <= row + yl * TOK
    for h in range(HEADS):
        rows = slice(h * TOK, (h + 1) * TOK)
        sc = jnp.where(allowed, dot_nt(qs[rows, :], kc) * (ROOT * LOG2E), -1e30)
        sbuf[c, rows, :] = sc
        stat[rows, :] = jnp.maximum(sc[:, :TOK], sc[:, TOK:])

    def scores(i):
        ch = c - 1 - i

        k_wait(2 * ch + 1 - yl)
        kc = keys_of(ch)
        for h in range(HEADS):
            rows = slice(h * TOK, (h + 1) * TOK)
            sc = dot_nt(qs[rows, :], kc) * (ROOT * LOG2E)
            sbuf[ch, rows, :] = sc
            stat[rows, :] = jnp.maximum(stat[rows, :], jnp.maximum(sc[:, :TOK], sc[:, TOK:]))

    paced(c, scores, 2)
    for h in range(HEADS):
        rows = slice(h * TOK, (h + 1) * TOK)
        stat[rows, :] = jnp.broadcast_to(jnp.max(stat[rows, :], axis=1, keepdims=True), (TOK, HEAD))
    linv[...] = jnp.zeros_like(linv)

    def exps(i):
        ch = c - i
        for h in range(HEADS):
            rows = slice(h * TOK, (h + 1) * TOK)
            m = stat[rows, :]
            e0 = jnp.exp2(sbuf[ch, rows, 0:TOK] - m)
            e1 = jnp.exp2(sbuf[ch, rows, TOK:2 * TOK] - m)
            linv[rows, :] += e0 + e1
            ebuf[ch, rows, 0:TOK] = e0.astype(BF16)
            ebuf[ch, rows, TOK:2 * TOK] = e1.astype(BF16)

    paced(c + 1, exps, 2)
    for h in range(HEADS):
        rows = slice(h * TOK, (h + 1) * TOK)
        inv = 1.0 / jnp.sum(linv[rows, :], axis=1, keepdims=True)
        linv[rows, :] = jnp.broadcast_to(inv, (TOK, HEAD))
        dol[rows, :] = (go[:, rows].astype(F32) * inv).astype(BF16)

    weights = dot_nt(uv[...], dol[...])
    w_hi, w_lo = split2(weights)
    w16 = jnp.concatenate([w_hi, w_lo], axis=0).astype(BF16)

    def lg_copy(to):
        return remote(lgout.at[to], lgin.at[p], ls.at[to], lr.at[p], dev(g, to))

    def grads(i):
        ch = c - i
        both = dot(w16, ebuf[ch])
        lg = GAIN * (both[0:RANK] + both[RANK:2 * RANK])
        lgout[2 * ch] = lg[:, 0:TOK]
        lgout[2 * ch + 1] = lg[:, TOK:2 * TOK]

        @pl.when(2 * ch < p)
        def _():
            lg_copy(2 * ch).start()

        @pl.when(2 * ch + 1 < p)
        def _():
            lg_copy(2 * ch + 1).start()

    paced(c + 1, grads, 4)

    oacc[...] = jnp.zeros_like(oacc)
    dqacc[...] = jnp.zeros_like(dqacc)

    def outs(i):
        ch = c - i

        @pl.when(i > 0)
        def _():
            v_wait(2 * ch)
            v_wait(2 * ch + 1)

        @pl.when(jnp.logical_and(i == 0, yl == 1))
        def _():
            v_wait(mate)

        vc = jnp.concatenate([vbuf[2 * ch, 0:TOK, :], vbuf[2 * ch + 1, 0:TOK, :]], axis=0)
        for h in range(HEADS):
            rows = slice(h * TOK, (h + 1) * TOK)
            oacc[rows, :] += dot(ebuf[ch, rows, :], vc)
            dpbuf[ch, rows, :] = dot_nt(go[:, rows], vc)

    paced(c + 1, outs, 4)
    for h in range(HEADS):
        rows = slice(h * TOK, (h + 1) * TOK)
        o = oacc[rows, :] * linv[rows, :]
        att[:, rows] = o.astype(BF16)
        center = jnp.sum(o * go[:, rows].astype(F32), axis=1, keepdims=True)
        stat[rows, :] = jnp.broadcast_to(center, (TOK, HEAD))

    unloads = [
        pltpu.make_async_copy(src, dst, unload.at[i])
        for i, (src, dst) in enumerate(((att, att_h), (gdq, gdq_h), (guq, guq_h), (gdv, gdv_h), (guv, guv_h)))
    ]
    unloads[0].start()

    def dquery(first, width):
        kc = kbuf[pl.ds(2 * first, 2 * width)].reshape(2 * width * TOK, HEAD)
        for h in range(HEADS):
            rows = slice(h * TOK, (h + 1) * TOK)
            cen = stat[rows, :]
            ds = []
            for j in range(width):
                for half in (slice(0, TOK), slice(TOK, 2 * TOK)):
                    part = dpbuf[first + j, rows, half] - cen
                    ds.append((ebuf[first + j, rows, half].astype(F32) * part).astype(BF16))
            dqacc[rows, :] += dot(jnp.concatenate(ds, axis=1), kc)

    def dquery_four(i, carry):
        dquery(4 * i, 4)
        return carry

    def dquery_one(i, carry):
        dquery(i, 1)
        return carry

    fours = (c + 1) // 4
    lax.fori_loop(0, fours, dquery_four, 0)
    lax.fori_loop(4 * fours, c + 1, dquery_one, 0)
    for h in range(HEADS):
        rows = slice(h * TOK, (h + 1) * TOK)
        d_hi, d_lo = split2(dqacc[rows, :] * (linv[rows, :] * ROOT))
        dqhi[:, rows] = d_hi.astype(BF16)
        dqlo[:, rows] = d_lo.astype(BF16)
    lgq = GAIN * (dot_nt(uq[...], dqhi[...]) + dot_nt(uq[...], dqlo[...]))

    def wait_lg(pp, acc):
        arrived(lgin.at[pp], lr.at[pp])
        return acc + lgin[pp]

    lgv = lax.fori_loop(p + 1, group, wait_lg, lgout[p])
    parts2[t] = jnp.concatenate([lgq, lgv], axis=0)

    def part2_copy(i):
        peer = lax.rem(t + i, n_tensor)
        return remote(parts2.at[t], parts2.at[t], p2s.at[0], p2r.at[0], (s, peer))

    def start_part2(i, carry):
        part2_copy(i).start()
        return carry

    lax.fori_loop(1, n_tensor, start_part2, 0)

    lq16 = jnp.concatenate([hi[:RANK], rest[:RANK]], axis=0).astype(BF16)
    g_up = dot(lq16, dqhi[...])
    g_lo = dot(lq16, dqlo[...])
    g_up_q = GAIN * (g_up[:RANK] + g_up[RANK:] + g_lo[:RANK])
    def lows(i, tt):
        ch = c - i
        low16 = jnp.concatenate([vbuf[2 * ch, TOK:TOK + 16, :], vbuf[2 * ch + 1, TOK:TOK + 16, :]], axis=1)
        return tt + dot_nt(low16, ebuf[ch])

    tt = lax.fori_loop(0, c + 1, lows, jnp.zeros((16, HEADS * TOK), F32))
    t_hi, t_lo = split2(tt[:RANK] + tt[RANK:])
    g_v = dot(jnp.concatenate([t_hi, t_lo], axis=0).astype(BF16), dol[...])
    g_up_v = GAIN * (g_v[:RANK] + g_v[RANK:])
    rank_row = lax.broadcasted_iota(jnp.int32, (RANK, HEAD), 0)
    for k in range(chips):
        aout[k, RANK:2 * RANK, :] = g_up_q[:, k * wide:(k + 1) * wide]
        if wide > HEAD:
            aout[k, 3 * RANK:4 * RANK, :] = jnp.zeros((RANK, wide), F32)
        aout[k, 3 * RANK:4 * RANK, 0:HEAD] = jnp.where(lax.rem(rank_row, chips) == k, g_up_v, 0.0)

    def end_row(to, carry):
        k_copy(to).wait_send()
        return carry

    def end_v(to, carry):
        v_copy(to).wait_send()
        return carry

    def end_pair(frm, carry):
        k_pair(frm).wait_send()
        return carry

    def end_lg(to, carry):
        lg_copy(to).wait_send()
        return carry

    arrived_all(parts1, p1s, n_tensor)
    lax.fori_loop(c + 1, chips, end_row, 0)
    lax.fori_loop(0, c + 1, end_pair, 0)
    lax.fori_loop(p + 1, group, end_v, 0)
    lax.fori_loop(0, p, end_lg, 0)

    arrived_all(parts2, p2r, n_tensor)
    lowg = parts2[0]
    for i in range(1, n_tensor):
        lowg = lowg + parts2[i]
    g_down = dot(lowg.astype(BF16), hid[...])
    for k in range(chips):
        aout[k, 0:RANK, :] = g_down[0:RANK, k * wide:(k + 1) * wide]
        aout[k, 2 * RANK:3 * RANK, :] = g_down[RANK:2 * RANK, k * wide:(k + 1) * wide]

    def a_copy(i):
        to = lax.rem(c + i, chips)
        return remote(aout.at[to], ain.at[c], asd.at[0], ard.at[0], dev(g, 2 * to + yl))

    def c_copy(i):
        to = lax.rem(c + i, chips)
        return remote(cin.at[c], cin.at[c], csd.at[0], crd.at[0], dev(g, 2 * to + yl))

    mine = 2 * g + yl

    def b_copy(i):
        slot = lax.rem(mine + i, 2 * n_groups)
        return remote(
            bin_.at[mine], bin_.at[mine], bsd.at[0], brd.at[0],
            dev(slot // 2, 2 * c + lax.rem(slot, 2)),
        )

    def start_a(i, carry):
        a_copy(i).start()
        return carry

    def start_b(i, carry):
        b_copy(i).start()
        return carry

    def start_c(i, carry):
        c_copy(i).start()
        return carry

    lax.fori_loop(1, chips, start_a, 0)
    ain[c] = aout[c]
    arrived_all(ain, ard, chips)
    total = ain[0]
    for k in range(1, chips):
        total = total + ain[k]
    bin_[mine] = total
    lax.fori_loop(1, 2 * n_groups, start_b, 0)
    arrived_all(bin_, brd, 2 * n_groups)
    total = bin_[0]
    for k in range(1, 2 * n_groups):
        total = total + bin_[k]
    cin[c] = total
    lax.fori_loop(1, chips, start_c, 0)

    arrived_all(parts2, p2s, n_tensor)
    arrived_all(aout, asd, chips)
    arrived_all(bin_, bsd, 2 * n_groups)
    arrived_all(cin, crd, chips)
    up_total = jnp.zeros((RANK, HEAD), F32)
    for k in range(chips):
        gdq[:, k * wide:(k + 1) * wide] = cin[k, 0:RANK, :]
        guq[:, k * wide:(k + 1) * wide] = cin[k, RANK:2 * RANK, :]
        gdv[:, k * wide:(k + 1) * wide] = cin[k, 2 * RANK:3 * RANK, :]
        up_total = up_total + cin[k, 3 * RANK:4 * RANK, 0:HEAD]
    guv[...] = up_total
    for copy in unloads[1:]:
        copy.start()
    arrived_all(cin, csd, chips)

    for copy in unloads:
        copy.wait()


def store(*refs):
    made, out, held, sem = refs[0:5], refs[5:10], refs[10:15], refs[15]
    copies = [pltpu.make_async_copy(made[i], held[i], sem.at[0, i]) for i in range(5)]
    backs = [pltpu.make_async_copy(held[i], out[i], sem.at[1, i]) for i in range(5)]
    for copy in copies:
        copy.start()
    for copy, back in zip(copies, backs):
        copy.wait()
        back.start()
    for back in backs:
        back.wait()


def solution(mesh, group_tokens=GROUP_TOKENS):
    n_seq, n_tensor = mesh.shape["seq"], mesh.shape["tensor"]
    group = group_tokens // TOK
    chips = group // 2
    far = 2 * (n_seq // group)
    wide = WIDTH // chips
    rows = HEADS * TOK
    dma = pltpu.SemaphoreType.DMA

    hbm = pl.BlockSpec(memory_space=pltpu.HBM)
    results = (
        jax.ShapeDtypeStruct((TOK, WIDTH), BF16),
        jax.ShapeDtypeStruct((RANK, WIDTH), F32),
        jax.ShapeDtypeStruct((RANK, WIDTH), F32),
        jax.ShapeDtypeStruct((RANK, WIDTH), F32),
        jax.ShapeDtypeStruct((RANK, HEAD), F32),
    )

    def per_device(*args):
        made = pl.pallas_call(
            functools.partial(kernel, n_seq, n_tensor, group),
            out_shape=results,
            in_specs=[hbm] * 9,
            out_specs=(hbm,) * 5,
            scratch_shapes=[pltpu.VMEM(a.shape, a.dtype) for a in results] + [dma((5,))]
            + [pltpu.VMEM(a.shape, a.dtype) for a in args] + [
                dma((9,)),
                pltpu.VMEM((n_tensor, 2 * RANK, TOK), F32),
                pltpu.VMEM((n_tensor, 2 * RANK, TOK), F32),
                pltpu.VMEM((group, TOK, HEAD), BF16),
                pltpu.VMEM((group, TOK + 16, HEAD), BF16),
                pltpu.VMEM((TOK + 16, HEAD), BF16),
                pltpu.VMEM((group, RANK, TOK), F32),
                pltpu.VMEM((group, RANK, TOK), F32),
                pltpu.VMEM((chips, 4 * RANK, wide), F32),
                pltpu.VMEM((far, 4 * RANK, wide), F32),
                pltpu.VMEM((chips, 4 * RANK, wide), F32),
                pltpu.VMEM((chips, 4 * RANK, wide), F32),
                pltpu.VMEM((rows, HEAD), BF16),
                pltpu.VMEM((chips, rows, 2 * TOK), F32),
                pltpu.VMEM((chips, rows, 2 * TOK), BF16),
                pltpu.VMEM((chips, rows, 2 * TOK), F32),
                pltpu.VMEM((rows, HEAD), F32),
                pltpu.VMEM((rows, HEAD), F32),
                pltpu.VMEM((rows, HEAD), F32),
                pltpu.VMEM((rows, HEAD), F32),
                pltpu.VMEM((rows, HEAD), BF16),
                pltpu.VMEM((TOK, WIDTH), BF16),
                pltpu.VMEM((TOK, WIDTH), BF16),
                dma((n_tensor,)), dma((n_tensor,)),
                dma((chips,)), dma((chips,)), dma((group,)),
                dma((group,)), dma((group,)),
                dma((group,)), dma((group,)),
                dma((n_tensor,)), dma((n_tensor,)),
                dma((chips,)), dma((chips,)),
                dma((far,)), dma((far,)),
                dma((chips,)), dma((chips,)),
            ],
            compiler_params=pltpu.CompilerParams(
                collective_id=0, has_side_effects=True, vmem_limit_bytes=60 * 1024 * 1024
            ),
        )(*args)
        return pl.pallas_call(
            store,
            out_shape=results,
            in_specs=[hbm] * 5,
            out_specs=(hbm,) * 5,
            scratch_shapes=[pltpu.VMEM(a.shape, a.dtype) for a in results] + [dma((2, 5))],
            compiler_params=pltpu.CompilerParams(vmem_limit_bytes=60 * 1024 * 1024),
        )(*made)

    split = P("seq", "tensor")
    cols = P(None, "tensor")
    return jax.shard_map(
        per_device,
        mesh=mesh,
        in_specs=(split, split, split, split, cols, cols, cols, cols, split),
        out_specs=(split, cols, cols, cols, cols),
        check_vma=False,
    )
```

```python
import functools
import math

import jax
import jax.numpy as jnp
from jax import lax
from jax.experimental import pallas as pl
from jax.experimental.pallas import tpu as pltpu
from jax.sharding import PartitionSpec as P

MESH = pl.DeviceIdType.MESH
GROUP_TOKENS = 2048
HEADS = 8
HEAD = 128
RANK = 8
TOK = 128
WIDTH = HEADS * HEAD
GAIN = 2.0
ROOT = HEAD ** -0.5
LOG2E = math.log2(math.e)
F32 = jnp.float32
BF16 = jnp.bfloat16
NT = (((1,), (1,)), ((), ()))


def paced(count, body, width):
    def step(i, carry):
        for j in range(width):
            body(i * width + j)
        return carry

    def rest(i, carry):
        body(i)
        return carry

    whole = count // width
    lax.fori_loop(0, whole, step, 0)
    lax.fori_loop(whole * width, count, rest, 0)


def arrived_all(buf, sem, count):
    if count > 1:
        arrived(buf.at[pl.ds(0, count - 1)], sem.at[0])


def dot(a, b):
    return jnp.dot(a, b, preferred_element_type=F32)


def dot_nt(a, b):
    return lax.dot_general(a, b, NT, preferred_element_type=F32)


def split2(x):
    hi = x.astype(BF16).astype(F32)
    return hi, x - hi


def arrived(buf, sem):
    pltpu.make_async_copy(buf, buf, sem).wait()


def kernel(
    n_seq, n_tensor, group,
    hid_h, qb_h, kp_h, fv_h, dq_h, uq_h, dv_h, uv_h, go_h,
    att_h, gdq_h, guq_h, gdv_h, guv_h,
    att, gdq, guq, gdv, guv, unload,
    hid, qb, kp, fv, dq, uq, dv, uv, go, load,
    parts1, parts2, kbuf, vbuf, vown, lgout, lgin, ain, bin_, cin, aout,
    qs, sbuf, ebuf, dpbuf, stat, linv, oacc, dqacc, dol, dqhi, dqlo,
    p1s, p1r, ks, kf, kr, vs, vr, ls, lr, p2s, p2r, asd, ard, bsd, brd, csd, crd,
):
    s = lax.axis_index("seq")
    t = lax.axis_index("tensor")
    chips = group // 2
    n_groups = n_seq // group
    wide = WIDTH // chips
    lag = jnp.where(t >= n_tensor // 2, group // 2, 0)
    rolled = lax.rem(s - lag + n_seq, n_seq)
    g = rolled // group
    p = lax.rem(rolled, group)
    c = p // 2
    yl = lax.rem(p, 2)
    mate = 2 * c + 1 - yl

    def place(gg, pp):
        return lax.rem(gg * group + pp + lag, n_seq)

    def dev(gg, pp):
        return (place(gg, pp), t)

    def remote(src, dst, send, recv, device):
        return pltpu.make_async_remote_copy(
            src_ref=src, dst_ref=dst, send_sem=send, recv_sem=recv,
            device_id=device, device_id_type=MESH,
        )

    loads = [
        pltpu.make_async_copy(src, dst, load.at[i])
        for i, (src, dst) in enumerate((
            (kp_h, kp), (hid_h, hid), (dq_h, dq), (dv_h, dv), (fv_h, fv), (uv_h, uv), (uq_h, uq), (qb_h, qb), (go_h, go),
        ))
    ]
    for copy in loads[:4]:
        copy.start()

    barrier = pltpu.get_barrier_semaphore()

    def greet(device):
        pl.semaphore_signal(barrier, inc=1, device_id=device, device_id_type=MESH)

    def greet_tensor(i, carry):
        greet((s, lax.rem(t + i, n_tensor)))
        return carry

    def greet_group(i, carry):
        greet(dev(g, lax.rem(p + i, group)))
        return carry

    def greet_far(i, carry):
        greet(dev(lax.rem(g + 1 + i // 2, n_groups), 2 * c + lax.rem(i, 2)))
        return carry

    lax.fori_loop(1, n_tensor, greet_tensor, 0)
    lax.fori_loop(1, group, greet_group, 0)
    lax.fori_loop(0, 2 * (n_groups - 1), greet_far, 0)

    for copy in loads[4:]:
        copy.start()
    loads[0].wait()
    kbuf[p] = kp[...]

    for copy in loads[1:4]:
        copy.wait()
    down = jnp.concatenate([dq[...].astype(F32), dv[...].astype(F32)], axis=0).astype(BF16)
    parts1[t] = dot_nt(down, hid[...])
    pl.semaphore_wait(barrier, (n_tensor - 1) + (group - 1) + 2 * (n_groups - 1))

    def part1_copy(i):
        peer = lax.rem(t + i, n_tensor)
        return remote(parts1.at[t], parts1.at[t], p1s.at[0], p1r.at[0], (s, peer))

    def start_part1(i, carry):
        part1_copy(i).start()
        return carry


    def k_copy(to):
        return remote(kp, kbuf.at[p], ks.at[to], kr.at[p], dev(g, 2 * to + yl))

    def k_pair(frm):
        return remote(kbuf.at[2 * frm + yl], kbuf.at[2 * frm + yl], kf.at[frm], kr.at[2 * frm + yl], dev(g, mate))

    def v_copy(to):
        return remote(vown, vbuf.at[p], vs.at[to], vr.at[p], dev(g, to))

    def k_wait(pp):
        arrived(kbuf.at[pp], kr.at[pp])

    def v_wait(pp):
        arrived(vbuf.at[pp], vr.at[pp])

    lax.fori_loop(1, n_tensor, start_part1, 0)
    def start_k(to, carry):
        k_copy(to).start()
        return carry

    lax.fori_loop(c + 1, chips, start_k, 0)
    k_pair(c).start()

    for copy in loads[4:]:
        copy.wait()

    def forward_k(i, carry):
        frm = c - 1 - i
        k_wait(2 * frm + yl)
        k_pair(frm).start()
        return carry

    lax.fori_loop(0, c, forward_k, 0)

    none_q = jnp.zeros((RANK, WIDTH), F32)
    none_v = jnp.zeros((RANK, HEAD), F32)
    uqf = uq[...].astype(F32)
    uvf = uv[...].astype(F32)
    up_v = jnp.concatenate([none_v, uvf] * 3 + [jnp.zeros((TOK - 48, HEAD), F32)], axis=0).astype(BF16)
    up_q = jnp.concatenate([uqf, none_q] * 3 + [jnp.zeros((TOK - 48, WIDTH), F32)], axis=0).astype(BF16)

    arrived_all(parts1, p1r, n_tensor)
    low = parts1[0]
    for i in range(1, n_tensor):
        low = low + parts1[i]
    hi = low.astype(BF16).astype(F32)
    rest = low - hi
    mid = rest.astype(BF16).astype(F32)
    lo = rest - mid
    zeros = jnp.zeros((TOK - 48, TOK), F32)
    pieces = jnp.transpose(jnp.concatenate([hi, mid, lo, zeros], axis=0)).astype(BF16)
    value = (fv[...].astype(F32) + GAIN * dot(pieces, up_v)).astype(BF16)
    low_v = jnp.concatenate([hi[RANK:], rest[RANK:]], axis=0).astype(BF16)
    vown[0:TOK, :] = value
    vown[TOK:TOK + 16, :] = low_v
    vbuf[p] = vown[...]

    @pl.when(yl == 0)
    def _():
        vbuf[mate] = jnp.zeros((TOK + 16, HEAD), BF16)


    def start_v(to, carry):
        v_copy(to).start()
        return carry

    lax.fori_loop(c + yl, chips, lambda i, q: start_v(2 * i + 1 - yl, q), 0)
    lax.fori_loop(c + 1, chips, lambda i, q: start_v(2 * i + yl, q), 0)

    for h in range(HEADS):
        cols = slice(h * HEAD, (h + 1) * HEAD)
        qs[cols, :] = (qb[:, cols].astype(F32) + GAIN * dot(pieces, up_q[:, cols])).astype(BF16)

    def keys_of(ch):
        return kbuf[pl.ds(2 * ch, 2)].reshape(2 * TOK, HEAD)

    k_wait(mate)
    kc = keys_of(c)
    column = lax.broadcasted_iota(jnp.int32, (TOK, 2 * TOK), 1)
    row = lax.broadcasted_iota(jnp.int32, (TOK, 2 * TOK), 0)
    allowed = column <= row + yl * TOK
    for h in range(HEADS):
        rows = slice(h * TOK, (h + 1) * TOK)
        sc = jnp.where(allowed, dot_nt(qs[rows, :], kc) * (ROOT * LOG2E), -1e30)
        sbuf[c, rows, :] = sc
        stat[rows, :] = jnp.maximum(sc[:, :TOK], sc[:, TOK:])

    def scores(i):
        ch = c - 1 - i

        k_wait(2 * ch + 1 - yl)
        kc = keys_of(ch)
        for h in range(HEADS):
            rows = slice(h * TOK, (h + 1) * TOK)
            sc = dot_nt(qs[rows, :], kc) * (ROOT * LOG2E)
            sbuf[ch, rows, :] = sc
            stat[rows, :] = jnp.maximum(stat[rows, :], jnp.maximum(sc[:, :TOK], sc[:, TOK:]))

    paced(c, scores, 4)
    for h in range(HEADS):
        rows = slice(h * TOK, (h + 1) * TOK)
        stat[rows, :] = jnp.broadcast_to(jnp.max(stat[rows, :], axis=1, keepdims=True), (TOK, HEAD))
    linv[...] = jnp.zeros_like(linv)

    def exps(i):
        ch = c - i
        for h in range(HEADS):
            rows = slice(h * TOK, (h + 1) * TOK)
            m = stat[rows, :]
            e0 = jnp.exp2(sbuf[ch, rows, 0:TOK] - m)
            e1 = jnp.exp2(sbuf[ch, rows, TOK:2 * TOK] - m)
            linv[rows, :] += e0 + e1
            ebuf[ch, rows, 0:TOK] = e0.astype(BF16)
            ebuf[ch, rows, TOK:2 * TOK] = e1.astype(BF16)

    paced(c + 1, exps, 2)
    for h in range(HEADS):
        rows = slice(h * TOK, (h + 1) * TOK)
        inv = 1.0 / jnp.sum(linv[rows, :], axis=1, keepdims=True)
        linv[rows, :] = jnp.broadcast_to(inv, (TOK, HEAD))
        dol[rows, :] = (go[:, rows].astype(F32) * inv).astype(BF16)

    weights = dot_nt(uv[...], dol[...])
    w_hi, w_lo = split2(weights)
    w16 = jnp.concatenate([w_hi, w_lo], axis=0).astype(BF16)

    def lg_copy(to):
        return remote(lgout.at[to], lgin.at[p], ls.at[to], lr.at[p], dev(g, to))

    def grads(i):
        ch = c - i
        both = dot(w16, ebuf[ch])
        lg = GAIN * (both[0:RANK] + both[RANK:2 * RANK])
        lgout[2 * ch] = lg[:, 0:TOK]
        lgout[2 * ch + 1] = lg[:, TOK:2 * TOK]

        @pl.when(2 * ch < p)
        def _():
            lg_copy(2 * ch).start()

        @pl.when(2 * ch + 1 < p)
        def _():
            lg_copy(2 * ch + 1).start()

    paced(c + 1, grads, 4)

    oacc[...] = jnp.zeros_like(oacc)
    dqacc[...] = jnp.zeros_like(dqacc)

    def outs(i):
        ch = c - i

        @pl.when(i > 0)
        def _():
            v_wait(2 * ch)
            v_wait(2 * ch + 1)

        @pl.when(jnp.logical_and(i == 0, yl == 1))
        def _():
            v_wait(mate)

        vc = jnp.concatenate([vbuf[2 * ch, 0:TOK, :], vbuf[2 * ch + 1, 0:TOK, :]], axis=0)
        for h in range(HEADS):
            rows = slice(h * TOK, (h + 1) * TOK)
            oacc[rows, :] += dot(ebuf[ch, rows, :], vc)
            dpbuf[ch, rows, :] = dot_nt(go[:, rows], vc)

    paced(c + 1, outs, 4)
    for h in range(HEADS):
        rows = slice(h * TOK, (h + 1) * TOK)
        o = oacc[rows, :] * linv[rows, :]
        att[:, rows] = o.astype(BF16)
        center = jnp.sum(o * go[:, rows].astype(F32), axis=1, keepdims=True)
        stat[rows, :] = jnp.broadcast_to(center, (TOK, HEAD))

    unloads = [
        pltpu.make_async_copy(src, dst, unload.at[i])
        for i, (src, dst) in enumerate(((att, att_h), (gdq, gdq_h), (guq, guq_h), (gdv, gdv_h), (guv, guv_h)))
    ]
    unloads[0].start()

    def dquery(first, width):
        kc = kbuf[pl.ds(2 * first, 2 * width)].reshape(2 * width * TOK, HEAD)
        for h in range(HEADS):
            rows = slice(h * TOK, (h + 1) * TOK)
            cen = stat[rows, :]
            ds = []
            for j in range(width):
                for half in (slice(0, TOK), slice(TOK, 2 * TOK)):
                    part = dpbuf[first + j, rows, half] - cen
                    ds.append((ebuf[first + j, rows, half].astype(F32) * part).astype(BF16))
            dqacc[rows, :] += dot(jnp.concatenate(ds, axis=1), kc)

    def dquery_four(i, carry):
        dquery(4 * i, 4)
        return carry

    def dquery_one(i, carry):
        dquery(i, 1)
        return carry

    fours = (c + 1) // 4
    lax.fori_loop(0, fours, dquery_four, 0)
    lax.fori_loop(4 * fours, c + 1, dquery_one, 0)
    for h in range(HEADS):
        rows = slice(h * TOK, (h + 1) * TOK)
        d_hi, d_lo = split2(dqacc[rows, :] * (linv[rows, :] * ROOT))
        dqhi[:, rows] = d_hi.astype(BF16)
        dqlo[:, rows] = d_lo.astype(BF16)
    lgq = GAIN * (dot_nt(uq[...], dqhi[...]) + dot_nt(uq[...], dqlo[...]))

    def wait_lg(pp, acc):
        arrived(lgin.at[pp], lr.at[pp])
        return acc + lgin[pp]

    lgv = lax.fori_loop(p + 1, group, wait_lg, lgout[p])
    parts2[t] = jnp.concatenate([lgq, lgv], axis=0)

    def part2_copy(i):
        peer = lax.rem(t + i, n_tensor)
        return remote(parts2.at[t], parts2.at[t], p2s.at[0], p2r.at[0], (s, peer))

    def start_part2(i, carry):
        part2_copy(i).start()
        return carry

    lax.fori_loop(1, n_tensor, start_part2, 0)

    lq16 = jnp.concatenate([hi[:RANK], rest[:RANK]], axis=0).astype(BF16)
    g_up = dot(lq16, dqhi[...])
    g_lo = dot(lq16, dqlo[...])
    g_up_q = GAIN * (g_up[:RANK] + g_up[RANK:] + g_lo[:RANK])
    def lows(i, tt):
        ch = c - i
        low16 = jnp.concatenate([vbuf[2 * ch, TOK:TOK + 16, :], vbuf[2 * ch + 1, TOK:TOK + 16, :]], axis=1)
        return tt + dot_nt(low16, ebuf[ch])

    tt = lax.fori_loop(0, c + 1, lows, jnp.zeros((16, HEADS * TOK), F32))
    t_hi, t_lo = split2(tt[:RANK] + tt[RANK:])
    g_v = dot(jnp.concatenate([t_hi, t_lo], axis=0).astype(BF16), dol[...])
    g_up_v = GAIN * (g_v[:RANK] + g_v[RANK:])
    rank_row = lax.broadcasted_iota(jnp.int32, (RANK, HEAD), 0)
    for k in range(chips):
        aout[k, RANK:2 * RANK, :] = g_up_q[:, k * wide:(k + 1) * wide]
        if wide > HEAD:
            aout[k, 3 * RANK:4 * RANK, :] = jnp.zeros((RANK, wide), F32)
        aout[k, 3 * RANK:4 * RANK, 0:HEAD] = jnp.where(lax.rem(rank_row, chips) == k, g_up_v, 0.0)

    def end_row(to, carry):
        k_copy(to).wait_send()
        return carry

    def end_v(to, carry):
        v_copy(to).wait_send()
        return carry

    def end_pair(frm, carry):
        k_pair(frm).wait_send()
        return carry

    def end_lg(to, carry):
        lg_copy(to).wait_send()
        return carry

    arrived_all(parts1, p1s, n_tensor)
    lax.fori_loop(c + 1, chips, end_row, 0)
    lax.fori_loop(0, c + 1, end_pair, 0)
    lax.fori_loop(p + 1, group, end_v, 0)
    lax.fori_loop(0, p, end_lg, 0)

    arrived_all(parts2, p2r, n_tensor)
    lowg = parts2[0]
    for i in range(1, n_tensor):
        lowg = lowg + parts2[i]
    g_down = dot(lowg.astype(BF16), hid[...])
    for k in range(chips):
        aout[k, 0:RANK, :] = g_down[0:RANK, k * wide:(k + 1) * wide]
        aout[k, 2 * RANK:3 * RANK, :] = g_down[RANK:2 * RANK, k * wide:(k + 1) * wide]

    def a_copy(i):
        to = lax.rem(c + i, chips)
        return remote(aout.at[to], ain.at[c], asd.at[0], ard.at[0], dev(g, 2 * to + yl))

    def c_copy(i):
        to = lax.rem(c + i, chips)
        return remote(cin.at[c], cin.at[c], csd.at[0], crd.at[0], dev(g, 2 * to + yl))

    mine = 2 * g + yl

    def b_copy(i):
        slot = lax.rem(mine + i, 2 * n_groups)
        return remote(
            bin_.at[mine], bin_.at[mine], bsd.at[0], brd.at[0],
            dev(slot // 2, 2 * c + lax.rem(slot, 2)),
        )

    def start_a(i, carry):
        a_copy(i).start()
        return carry

    def start_b(i, carry):
        b_copy(i).start()
        return carry

    def start_c(i, carry):
        c_copy(i).start()
        return carry

    lax.fori_loop(1, chips, start_a, 0)
    ain[c] = aout[c]
    arrived_all(ain, ard, chips)
    total = ain[0]
    for k in range(1, chips):
        total = total + ain[k]
    bin_[mine] = total
    lax.fori_loop(1, 2 * n_groups, start_b, 0)
    arrived_all(bin_, brd, 2 * n_groups)
    total = bin_[0]
    for k in range(1, 2 * n_groups):
        total = total + bin_[k]
    cin[c] = total
    lax.fori_loop(1, chips, start_c, 0)

    arrived_all(parts2, p2s, n_tensor)
    arrived_all(aout, asd, chips)
    arrived_all(bin_, bsd, 2 * n_groups)
    arrived_all(cin, crd, chips)
    up_total = jnp.zeros((RANK, HEAD), F32)
    for k in range(chips):
        gdq[:, k * wide:(k + 1) * wide] = cin[k, 0:RANK, :]
        guq[:, k * wide:(k + 1) * wide] = cin[k, RANK:2 * RANK, :]
        gdv[:, k * wide:(k + 1) * wide] = cin[k, 2 * RANK:3 * RANK, :]
        up_total = up_total + cin[k, 3 * RANK:4 * RANK, 0:HEAD]
    guv[...] = up_total
    for copy in unloads[1:]:
        copy.start()
    arrived_all(cin, csd, chips)

    for copy in unloads:
        copy.wait()


def store(*refs):
    made, out, held, sem = refs[0:5], refs[5:10], refs[10:15], refs[15]
    copies = [pltpu.make_async_copy(made[i], held[i], sem.at[0, i]) for i in range(5)]
    backs = [pltpu.make_async_copy(held[i], out[i], sem.at[1, i]) for i in range(5)]
    for copy in copies:
        copy.start()
    for copy, back in zip(copies, backs):
        copy.wait()
        back.start()
    for back in backs:
        back.wait()


def solution(mesh, group_tokens=GROUP_TOKENS):
    n_seq, n_tensor = mesh.shape["seq"], mesh.shape["tensor"]
    group = group_tokens // TOK
    chips = group // 2
    far = 2 * (n_seq // group)
    wide = WIDTH // chips
    rows = HEADS * TOK
    dma = pltpu.SemaphoreType.DMA

    hbm = pl.BlockSpec(memory_space=pltpu.HBM)
    results = (
        jax.ShapeDtypeStruct((TOK, WIDTH), BF16),
        jax.ShapeDtypeStruct((RANK, WIDTH), F32),
        jax.ShapeDtypeStruct((RANK, WIDTH), F32),
        jax.ShapeDtypeStruct((RANK, WIDTH), F32),
        jax.ShapeDtypeStruct((RANK, HEAD), F32),
    )

    def per_device(*args):
        made = pl.pallas_call(
            functools.partial(kernel, n_seq, n_tensor, group),
            out_shape=results,
            in_specs=[hbm] * 9,
            out_specs=(hbm,) * 5,
            scratch_shapes=[pltpu.VMEM(a.shape, a.dtype) for a in results] + [dma((5,))]
            + [pltpu.VMEM(a.shape, a.dtype) for a in args] + [
                dma((9,)),
                pltpu.VMEM((n_tensor, 2 * RANK, TOK), F32),
                pltpu.VMEM((n_tensor, 2 * RANK, TOK), F32),
                pltpu.VMEM((group, TOK, HEAD), BF16),
                pltpu.VMEM((group, TOK + 16, HEAD), BF16),
                pltpu.VMEM((TOK + 16, HEAD), BF16),
                pltpu.VMEM((group, RANK, TOK), F32),
                pltpu.VMEM((group, RANK, TOK), F32),
                pltpu.VMEM((chips, 4 * RANK, wide), F32),
                pltpu.VMEM((far, 4 * RANK, wide), F32),
                pltpu.VMEM((chips, 4 * RANK, wide), F32),
                pltpu.VMEM((chips, 4 * RANK, wide), F32),
                pltpu.VMEM((rows, HEAD), BF16),
                pltpu.VMEM((chips, rows, 2 * TOK), F32),
                pltpu.VMEM((chips, rows, 2 * TOK), BF16),
                pltpu.VMEM((chips, rows, 2 * TOK), F32),
                pltpu.VMEM((rows, HEAD), F32),
                pltpu.VMEM((rows, HEAD), F32),
                pltpu.VMEM((rows, HEAD), F32),
                pltpu.VMEM((rows, HEAD), F32),
                pltpu.VMEM((rows, HEAD), BF16),
                pltpu.VMEM((TOK, WIDTH), BF16),
                pltpu.VMEM((TOK, WIDTH), BF16),
                dma((n_tensor,)), dma((n_tensor,)),
                dma((chips,)), dma((chips,)), dma((group,)),
                dma((group,)), dma((group,)),
                dma((group,)), dma((group,)),
                dma((n_tensor,)), dma((n_tensor,)),
                dma((chips,)), dma((chips,)),
                dma((far,)), dma((far,)),
                dma((chips,)), dma((chips,)),
            ],
            compiler_params=pltpu.CompilerParams(
                collective_id=0, has_side_effects=True, vmem_limit_bytes=60 * 1024 * 1024
            ),
        )(*args)
        return pl.pallas_call(
            store,
            out_shape=results,
            in_specs=[hbm] * 5,
            out_specs=(hbm,) * 5,
            scratch_shapes=[pltpu.VMEM(a.shape, a.dtype) for a in results] + [dma((2, 5))],
            compiler_params=pltpu.CompilerParams(vmem_limit_bytes=60 * 1024 * 1024),
        )(*made)

    split = P("seq", "tensor")
    cols = P(None, "tensor")
    return jax.shard_map(
        per_device,
        mesh=mesh,
        in_specs=(split, split, split, split, cols, cols, cols, cols, split),
        out_specs=(split, cols, cols, cols, cols),
        check_vma=False,
    )
```
